512 devices in a mesh: parts: 512 (over x, z, y, core).
Axes of the slice: x: 4, y: 8, z: 8, core: 2. Of those that a mesh axis runs over, the one named last changes fastest.
Arguments:
- rhs_partial: float32 [3, 739840], P(None, 'parts'), may hold values from -12 to 12
- connectivity: int32 [27, 65536], P(None, 'parts'), may hold values from 0 to 1444, as said below
- hessians: bfloat16 [45, 27, 65536], P(None, None, 'parts'), may hold values from -1 to 3, as said below
- shared_nodes: int32 [8, 17408], P(None, 'parts'), may hold values from 0 to 1445, as said below
- owner: int32 [739840], P('parts'), may hold values from 0 to 1, as said below
Outputs:
- solution: float32 [3, 739840], P(None, 'parts')
- residual: float32 [3, 739840], P(None, 'parts')
The draws below stay inside these ranges and needn't reach their ends.
Inputs may be any that keep to these rules, and one draw needn't show every extreme that they name: `connectivity`: local node numbers of the element's own partition; each partition's elements form a conforming block of 8 x 8 x 2 elements that share their common nodes. `hessians`: each 9 x 9 matrix is positive definite. `shared_nodes`: the rows of two neighbouring partitions for each other name the same physical nodes in the same order and are equally long; a local node is in at most one row, and only nodes on the block's boundary are in rows; used slots come first and unused slots hold 1445; in every draw some row of some partition has all 34 slots used. `owner`: 1 on every node in no row of shared_nodes, and on exactly one of the two copies of each shared node.
All inputs are finite; a program needn't handle non-finite values.
Results may differ from the reference program's by a relative error of at most 0.0003.
Values sent between devices are 32-bit elements; how exact they have to be, the bound alone decides.
A program may use at most 64 MiB of HBM per device.

```python
import math
import jax
import jax.numpy as jnp
import numpy as np
from jax import lax

EX = 8
EY = 8
EZ = 2
E_DEV = 128
NODE_DEV = 1445
SHARE = 34
PEERS = 8
ITERS = 5
ELEMS = 65536
NODES = 739840
N_PARTS = 512


def block_regions():
    first_count = 2 * EX + 1
    second_count = 2 * EY + 1
    third_count = 2 * EZ + 1
    first, second, third = np.meshgrid(np.arange(first_count), np.arange(second_count), np.arange(third_count), indexing='ij')
    first = first.reshape(-1)
    second = second.reshape(-1)
    third = third.reshape(-1)
    region = np.full(first.shape, 8)
    tests = [(first == 0) & (third < EZ), first == 0, (first == first_count - 1) & (third < EZ), first == first_count - 1, second == 0, second == second_count - 1, third == 0, third == third_count - 1]
    for region_index in range(8):
        region = np.where((region == 8) & tests[region_index], region_index, region)
    positions = np.arange(region.shape[0])
    return [positions[region == region_index].astype(np.int32) for region_index in range(8)]


def element_table():
    second_count = 2 * EY + 1
    third_count = 2 * EZ + 1
    first, second, third = np.meshgrid(np.arange(EX), np.arange(EY), np.arange(EZ), indexing='ij')
    rows = []
    for node_a in range(27):
        offset_first = node_a // 9
        offset_second = node_a // 3 % 3
        offset_third = node_a % 3
        number = ((2 * first + offset_first) * second_count + (2 * second + offset_second)) * third_count + (2 * third + offset_third)
        rows.append(number.reshape(-1))
    return np.stack(rows, 0).astype(np.int32)


def node_labels(key):
    label_key = jax.random.fold_in(key, 211)
    part_keys = jax.random.split(label_key, N_PARTS)
    return jax.vmap(lambda part_key: jax.random.permutation(part_key, NODE_DEV))(part_keys).astype(jnp.int32)


def share_layout(key):
    labels = node_labels(key)
    keys = jax.random.split(jax.random.fold_in(key, 101), 4)
    half = PEERS // 2
    regions = block_regions()
    counts = jax.random.randint(keys[1], (N_PARTS, half), SHARE // 4, SHARE + 1).astype(jnp.int32)
    fullest = jax.random.randint(keys[2], (), 0, N_PARTS).astype(jnp.int32)
    counts = jnp.where(jnp.arange(N_PARTS, dtype=jnp.int32)[:, None] == fullest, SHARE, counts)
    lower_owns = jax.random.randint(keys[3], (N_PARTS, half, SHARE), 0, 2).astype(jnp.int32)
    slot_index = jnp.arange(SHARE, dtype=jnp.int32)
    part_index = jnp.arange(N_PARTS, dtype=jnp.int32)
    rows = []
    owned_rows = []
    for row_index in range(PEERS):
        region_nodes = jnp.asarray(regions[row_index], dtype=jnp.int32)
        region_size = regions[row_index].shape[0]
        row_keys = jax.random.split(jax.random.fold_in(keys[0], row_index), N_PARTS)
        orders = jax.vmap(lambda row_key: jax.random.permutation(row_key, region_size))(row_keys).astype(jnp.int32)
        picked = jnp.take(region_nodes, orders[:, :SHARE], axis=0)
        region = jnp.take_along_axis(labels, picked, axis=1)
        if row_index < half:
            distance = half - row_index
            lower = (part_index - distance) % N_PARTS
            used = counts[lower, distance - 1]
            owns = 1 - lower_owns[lower, distance - 1]
        else:
            distance = row_index - half + 1
            used = counts[:, distance - 1]
            owns = lower_owns[:, distance - 1]
        live = slot_index[None, :] < used[:, None]
        rows.append(jnp.where(live, region, NODE_DEV))
        owned_rows.append(owns)
    lists = jnp.stack(rows, 1)
    owned_values = jnp.stack(owned_rows, 1)

    def mark(slots, values):
        return jnp.ones((NODE_DEV,), jnp.int32).at[slots.reshape(-1)].set(values.reshape(-1), mode='drop')
    owner = jax.vmap(mark)(lists, owned_values)
    return (lists, owner)


def draw_shared_nodes(key, part):
    lists, owner = share_layout(key)
    return jnp.transpose(lists, (1, 0, 2)).reshape(PEERS, SHARE * N_PARTS).astype(jnp.int32)


def draw_owner(key, part):
    lists, owner = share_layout(key)
    return owner.reshape(NODES).astype(jnp.int32)


def draw_connectivity(key, part):
    labels = node_labels(key)
    key = jax.random.fold_in(key, 5)
    table = jnp.asarray(element_table(), dtype=jnp.int32)
    part_keys = jax.random.split(key, N_PARTS)
    orders = jax.vmap(lambda part_key: jax.random.permutation(part_key, E_DEV))(part_keys).astype(jnp.int32)

    def one_part(part_labels, order):
        structured = jnp.take(table, order, axis=1)
        return jnp.take(part_labels, structured, axis=0)
    nodes = jax.vmap(one_part)(labels, orders)
    return jnp.transpose(nodes, (1, 0, 2)).reshape(27, ELEMS).astype(jnp.int32)


def draw_rhs_partial(key, part):
    key = jax.random.fold_in(key, 3)
    fraction = (jnp.arange(NODES, dtype=jnp.int32) // NODE_DEV).astype(jnp.float32) / (N_PARTS - 1)
    amplitude = jnp.exp(fraction * math.log(2.0))
    values = jnp.clip(jax.random.normal(key, (3, NODES), jnp.float32), -6.0, 6.0)
    return (values * amplitude[None, :]).astype(jnp.float32)


def draw_hessians(key, part):
    key = jax.random.fold_in(key, 7)
    log_span = math.log(10.0)
    shape = (27, ELEMS)
    diagonal = [0.1 * jnp.exp(jax.random.uniform(jax.random.fold_in(key, row_index), shape, jnp.float32, 0.0, log_span)) for row_index in range(9)]
    entries = []
    for row_index in range(9):
        for col_index in range(row_index, 9):
            if row_index == col_index:
                entries.append(diagonal[row_index].astype(jnp.bfloat16))
            else:
                entry_key = jax.random.fold_in(key, 100 + row_index * 9 + col_index)
                coupling = 0.11 * jnp.tanh(jax.random.normal(entry_key, shape, jnp.float32))
                entries.append((coupling * jnp.sqrt(diagonal[row_index] * diagonal[col_index])).astype(jnp.bfloat16))
    return jnp.stack(entries, 0)


def setup_inputs(seed: int = 0) -> dict:
    key_list = jax.random.split(jax.random.key(seed), 6)
    return {
        "rhs_partial": draw_rhs_partial(jax.random.fold_in(key_list[5], 71), 0),
        "connectivity": draw_connectivity(jax.random.fold_in(key_list[5], 71), 0),
        "hessians": draw_hessians(jax.random.fold_in(key_list[5], 71), 0),
        "shared_nodes": draw_shared_nodes(jax.random.fold_in(key_list[5], 71), 0),
        "owner": draw_owner(jax.random.fold_in(key_list[5], 71), 0),
    }


DAMPING = 2.0

def shape_table():
    points = np.array([-np.sqrt(0.6), 0.0, np.sqrt(0.6)])
    values = np.stack([points * (points - 1.0) / 2.0, 1.0 - points * points, points * (points + 1.0) / 2.0], axis=1)
    slopes = np.stack([points - 0.5, -2.0 * points, points + 0.5], axis=1)
    result = np.zeros((27, 3, 27))
    for direction in range(3):
        factors = [slopes if axis_index == direction else values for axis_index in range(3)]
        product = factors[0][:, None, None, :, None, None] * factors[1][None, :, None, None, :, None] * factors[2][None, None, :, None, None, :]
        result[:, direction, :] = product.reshape(27, 27)
    return jnp.asarray(result.reshape(81, 27), dtype=jnp.float32)

def packed_index(row_index, col_index):
    first = min(row_index, col_index)
    second = max(row_index, col_index)
    return first * 9 - first * (first - 1) // 2 + (second - first)

def apply_local(field, element_nodes, element_hessians):
    table = shape_table()
    elements = element_nodes.shape[1]
    node_count = field.shape[1]
    element_values = jnp.take(field, element_nodes, axis=1)
    element_values = jnp.transpose(element_values, (1, 0, 2)).reshape(27, 3 * elements)
    gradients = jnp.dot(table, element_values, precision=lax.Precision.HIGHEST).reshape(27, 3, 3, elements)
    components = [gradients[:, col_index % 3, col_index // 3, :] for col_index in range(9)]
    entries = [element_hessians[entry].astype(jnp.float32) for entry in range(45)]
    stresses = []
    for row_index in range(9):
        accumulated = entries[packed_index(row_index, 0)] * components[0]
        for col_index in range(1, 9):
            accumulated = accumulated + entries[packed_index(row_index, col_index)] * components[col_index]
        stresses.append(accumulated)
    stress = jnp.stack(stresses, 0).reshape(3, 3, 27, elements)
    stress = jnp.transpose(stress, (2, 1, 0, 3)).reshape(81, 3 * elements)
    element_terms = jnp.dot(table.T, stress, precision=lax.Precision.HIGHEST).reshape(27, 3, elements)
    summed = jnp.zeros((3, node_count), jnp.float32)
    return summed.at[:, element_nodes].add(jnp.transpose(element_terms, (1, 0, 2)))

def peer_offsets(count):
    half = count // 2
    return [offset - half for offset in range(half)] + [offset + 1 for offset in range(half)]

def reference(rhs_partial, connectivity, hessians, shared_nodes, owner):
    offsets = peer_offsets(PEERS)
    shared_lists = jnp.transpose(shared_nodes.reshape(PEERS, N_PARTS, SHARE), (1, 0, 2))
    owned_mask = owner.reshape(N_PARTS, NODE_DEV).astype(jnp.float32)

    def to_local(field):
        return jnp.transpose(field.reshape(3, N_PARTS, NODE_DEV), (1, 0, 2))

    def assemble(partial_value):
        outgoing = jax.vmap(lambda values, slots: jnp.take(values, slots, axis=1, mode='fill', fill_value=0.0))(partial_value, shared_lists)
        outgoing = jnp.transpose(outgoing, (0, 2, 1, 3))
        incoming = jnp.stack([jnp.roll(outgoing[:, PEERS - 1 - row_index], -offsets[row_index], axis=0) for row_index in range(PEERS)], 1)

        def add_one(values, slots, arriving):
            return values.at[:, slots].add(jnp.transpose(arriving, (1, 0, 2)), mode='drop')
        return jax.vmap(add_one)(partial_value, shared_lists, incoming)

    def operator(field):

        def one_part(part_index):
            element_nodes = lax.dynamic_slice_in_dim(connectivity, part_index * E_DEV, E_DEV, 1)
            element_hessians = lax.dynamic_slice_in_dim(hessians, part_index * E_DEV, E_DEV, 2)
            return apply_local(field[part_index], element_nodes, element_hessians)
        partial_value = lax.map(one_part, jnp.arange(N_PARTS, dtype=jnp.int32))
        return assemble(partial_value) + DAMPING * field

    def inner(first_field, second_field):
        return jnp.sum(owned_mask[:, None, :] * first_field * second_field)
    rhs = assemble(to_local(rhs_partial))
    solution = jnp.zeros_like(rhs)
    residual = rhs
    direction = rhs
    norm_now = inner(residual, residual)
    for iteration in range(ITERS):
        image = operator(direction)
        step_size = norm_now / inner(direction, image)
        solution = solution + step_size * direction
        residual = residual - step_size * image
        norm_next = inner(residual, residual)
        direction = residual + norm_next / norm_now * direction
        norm_now = norm_next

    def to_global(field):
        return jnp.transpose(field, (1, 0, 2)).reshape(3, NODES)
    return (to_global(solution), to_global(residual))
```

```python
import functools

import jax
import jax.numpy as jnp
import ml_dtypes
import numpy as np
from jax import lax
from jax.experimental import pallas as pl
from jax.experimental.pallas import tpu as pltpu
from jax.sharding import PartitionSpec as P

ITERS = 5
DAMPING = 2.0
MESH = pl.DeviceIdType.MESH
F32 = jnp.float32
BF16 = jnp.bfloat16

NODES = 1445
NODE_ROWS = 12
ROWS = 24
PEERS = 8
SHARE = 34
SHIFT_SCALE = 0.045


def shape_table():
    points = np.array([-np.sqrt(0.6), 0.0, np.sqrt(0.6)])
    values = np.stack(
        [points * (points - 1.0) / 2.0, 1.0 - points * points, points * (points + 1.0) / 2.0],
        axis=1,
    )
    slopes = np.stack([points - 0.5, -2.0 * points, points + 0.5], axis=1)
    result = np.zeros((27, 3, 27))
    for direction in range(3):
        factors = [slopes if axis_index == direction else values for axis_index in range(3)]
        product = (
            factors[0][:, None, None, :, None, None]
            * factors[1][None, :, None, None, :, None]
            * factors[2][None, None, :, None, None, :]
        )
        result[:, direction, :] = product.reshape(27, 27)
    return result


def three_parts(table):
    rest = table.astype(np.float32)
    parts = []
    for _ in range(3):
        part = rest.astype(ml_dtypes.bfloat16)
        parts.append(part)
        rest = rest - part.astype(np.float32)
    return parts


def tables():
    table = shape_table()
    forward = np.zeros((3, 32, 32))
    forward[:, :27, :27] = table.transpose(1, 0, 2)
    high, mid, low = three_parts(forward.reshape(96, 32))
    first = np.concatenate([high, high, high, mid, mid, low], axis=1)
    weights = np.einsum("qda,qfa->dfq", table, table)
    row = np.zeros((16, 6, 32))
    for pair, (one, two) in enumerate(PAIRS):
        row[0, pair, :27] = weights[one, two] * (1.0 if one == two else 2.0)
    first = np.concatenate([first, row.reshape(16, 192).astype(ml_dtypes.bfloat16)], axis=0)
    high, mid, low = three_parts(forward.transpose(2, 0, 1).reshape(32, 96))
    zero = np.zeros_like(high)
    second = np.concatenate(
        [
            np.concatenate([high, high, high], axis=1),
            np.concatenate([mid, mid, zero], axis=1),
            np.concatenate([low, zero, zero], axis=1),
        ],
        axis=0,
    )
    return first, second


PAIRS = [(0, 0), (0, 1), (0, 2), (1, 1), (1, 2), (2, 2)]


def packed_index(row_index, col_index):
    first = min(row_index, col_index)
    second = max(row_index, col_index)
    return first * 9 - first * (first - 1) // 2 + (second - first)


def peer_offsets(count):
    half = count // 2
    return [offset - half for offset in range(half)] + [offset + 1 for offset in range(half)]


def stage_digits(count):
    if count == 512:
        return [[(1, 2), (2, 8)], [(16, 8), (128, 4)]]
    small = 1
    while small * small < count:
        small *= 2
    return [[(1, small)], [(small, count // small)]]


def partners(me, digits):
    size = int(np.prod([digit for _, digit in digits]))
    place, scale, base = 0, 1, me
    for stride, digit in digits:
        value = lax.rem(lax.div(me, stride), digit)
        place = place + value * scale
        scale *= digit
        base = base - value * stride
    result = []
    for step in range(1, size):
        other = lax.rem(place + step, size)
        number = base
        for stride, digit in digits:
            number = number + lax.rem(other, digit) * stride
            other = lax.div(other, digit)
        result.append(number)
    return result


def parts_of(value):
    high = value.astype(BF16).astype(F32)
    rest = value - high
    mid = rest.astype(BF16).astype(F32)
    return high, mid, (rest - mid).astype(BF16).astype(F32)


def lane_of(row, lane):
    return jnp.broadcast_to(row[:, lane : lane + 1], (1, 128))


def spread(ref, row):
    return jnp.broadcast_to(ref[pl.ds(row, 1), :], (8, 128))


def pick(ref, base, count, first, rows, lanes, start):
    result = start
    for row in range(count):
        found = jnp.take_along_axis(spread(ref, base + row), lanes, axis=1)
        result = jnp.where(rows == first + row, found, result)
    return result


def kernel(
    count,
    rhs_ref,
    conn_ref,
    hess_ref,
    shared_ref,
    owner_ref,
    first_ref,
    second_ref,
    out_ref,
    nodes_scr,
    owner_scr,
    shared_scr,
    map_scr,
    conn_scr,
    row_scr,
    lane_scr,
    hot_scr,
    h_scr,
    q_scr,
    own_scr,
    inner_scr,
    in_scr,
    part_scr,
    u_scr,
    g_scr,
    s_scr,
    t_scr,
    rs_scr,
    ri_scr,
    weight_scr,
    moment_scr,
    scale_scr,
    basis_scr,
    send_buf,
    recv_buf,
    sum_out,
    sum_in0,
    sum_in1,
    halo_send,
    halo_recv,
    sum_send,
    sum_recv,
):
    me = lax.axis_index("parts")
    peers = [lax.rem(me + offset + count, count) for offset in peer_offsets(PEERS)]
    stages = [partners(me, digits) for digits in stage_digits(count)]
    sum_in = [sum_in0, sum_in1]

    barrier = pltpu.get_barrier_semaphore()
    everyone = peers + stages[0] + stages[1]
    for other in everyone:
        pl.semaphore_signal(barrier, inc=1, device_id=(other,), device_id_type=MESH)

    sublane = lax.broadcasted_iota(jnp.int32, (8, 128), 0)
    lane = lax.broadcasted_iota(jnp.int32, (8, 128), 1)
    sublane16 = lax.broadcasted_iota(jnp.int32, (16, 128), 0)

    def send_halo(turn):
        for j in range(PEERS):
            pltpu.make_async_remote_copy(
                src_ref=send_buf.at[turn, j],
                dst_ref=recv_buf.at[turn, PEERS - 1 - j],
                send_sem=halo_send.at[turn],
                recv_sem=halo_recv.at[turn],
                device_id=(peers[j],),
                device_id_type=MESH,
            ).start()

    def wait_halo(turn):
        pltpu.make_async_copy(recv_buf.at[turn], recv_buf.at[turn], halo_recv.at[turn]).wait()

    def send_sum(which, stage, row):
        slot = 2 * which + stage
        sum_out[slot] = row
        for k, other in enumerate(stages[stage]):
            pltpu.make_async_remote_copy(
                src_ref=sum_out.at[slot],
                dst_ref=sum_in[stage].at[which, k],
                send_sem=sum_send.at[slot],
                recv_sem=sum_recv.at[slot],
                device_id=(other,),
                device_id_type=MESH,
            ).start()

    def wait_sum(which, stage):
        slot = 2 * which + stage
        arrived = sum_in[stage].at[which]
        pltpu.make_async_copy(arrived, arrived, sum_recv.at[slot]).wait()
        terms = [sum_out[slot]] + [sum_in[stage][which, k] for k in range(len(stages[stage]))]
        while len(terms) > 1:
            terms = [sum(terms[i : i + 2]) for i in range(0, len(terms), 2)]
        return terms[0]

    nodes_scr[...] = jnp.zeros_like(nodes_scr)
    owner_scr[...] = jnp.zeros_like(owner_scr)
    for r in range(NODE_ROWS):
        width = min(128, NODES - 128 * r)
        for c in range(3):
            nodes_scr[pl.ds(16 * c + r, 1), 0:width] = rhs_ref[c : c + 1, 128 * r : 128 * r + width]
        owner_scr[pl.ds(r, 1), 0:width] = owner_ref[0:1, 128 * r : 128 * r + width].astype(F32)
    shared_scr[...] = jnp.full((8, 128), NODES, jnp.int32)
    shared_scr[:, 0:SHARE] = shared_ref[...]
    names = shared_scr[...]
    used = names < NODES
    name_rows, name_lanes = names >> 7, names & 127
    zero = jnp.zeros((8, 128), F32)
    for c in range(3):
        found = pick(nodes_scr, 16 * c, NODE_ROWS, 0, name_rows, name_lanes, zero)
        own_scr[pl.ds(8 * c, 8), :] = jnp.where(used, found, 0.0)
    weight_scr[0:8, :] = jnp.where(
        used, pick(owner_scr, 0, NODE_ROWS, 0, name_rows, name_lanes, zero), 0.0
    )

    def fill_message(turn):
        for c in range(3):
            for j in range(PEERS):
                send_buf[turn, j, c] = own_scr[pl.ds(8 * c + j, 1), :]

    fill_message(0)
    pl.semaphore_wait(barrier, len(everyone))
    send_halo(0)

    for k in range(45):
        h_scr[k, 24:32, :] = jnp.zeros((8, 128), F32)
        h_scr[k, 0:27, :] = hess_ref[k].astype(F32)
    sums = []
    for one, two in PAIRS:
        total = h_scr[packed_index(one, two)]
        for i in range(1, 3):
            total = total + h_scr[packed_index(3 * i + one, 3 * i + two)]
        sums.append(total)
    stacked = jnp.concatenate(sums, axis=0).astype(BF16)
    traces = jnp.dot(first_ref[96:112, :], stacked, preferred_element_type=F32)[0:1, :]

    def row_of(values):
        totals = jnp.sum(values, axis=1, keepdims=True)
        rows = lax.broadcasted_iota(jnp.int32, values.shape, 0)
        lanes = lax.broadcasted_iota(jnp.int32, values.shape, 1)
        return jnp.sum(jnp.where(rows == lanes, totals, 0.0), axis=0, keepdims=True)

    both = jnp.where(sublane == 0, traces, jnp.where(sublane == 1, traces * traces, 0.0))
    send_sum(0, 0, row_of(both))

    found = jnp.zeros((32, 128), F32)
    for j in range(PEERS):
        rows_j = jnp.broadcast_to(jnp.where(used, name_rows, 99)[j : j + 1, :], (16, 128))
        lanes_j = jnp.broadcast_to(name_lanes[j : j + 1, :], (128, 128))
        hit = rows_j == sublane16
        slot = lax.broadcasted_iota(jnp.int32, (16, 128), 1).astype(F32)
        left = jnp.concatenate(
            [jnp.where(hit, float(j + 1), 0.0), jnp.where(hit, slot, 0.0)], axis=0
        )
        right = jnp.where(
            lanes_j == lax.broadcasted_iota(jnp.int32, (128, 128), 0), 1.0, 0.0
        )
        found = found + lax.dot_general(
            left.astype(BF16),
            right.astype(BF16),
            (((1,), (1,)), ((), ())),
            preferred_element_type=F32,
        )
    map_scr[...] = (64.0 * found[0:16] + found[16:32]).astype(jnp.int32)
    weight_scr[8:24, :] = jnp.where(map_scr[...] > 0, 0.0, owner_scr[...])

    conn_scr[...] = jnp.zeros_like(conn_scr)
    conn_scr[0:27, :] = conn_ref[...]
    for t in range(4):
        names_t = conn_scr[pl.ds(8 * t, 8), :]
        rows_t, lanes_t = names_t >> 7, names_t & 127
        where_t = pick(map_scr, 0, NODE_ROWS, 0, rows_t, lanes_t, jnp.zeros((8, 128), jnp.int32))
        is_shared = where_t > 0
        row_t = jnp.where(is_shared, (where_t >> 6) - 1, rows_t + 8)
        if t == 3:
            row_t = jnp.where(sublane < 3, row_t, 99)
        row_scr[pl.ds(8 * t, 8), :] = row_t
        lane_scr[pl.ds(8 * t, 8), :] = jnp.where(is_shared, where_t & 63, lanes_t)

    columns = jnp.transpose(lane_scr[...].astype(F32))
    lanes_all = lax.broadcasted_iota(jnp.int32, (128, 128), 1).astype(F32)
    for a in range(27):
        column = jnp.broadcast_to(columns[:, a : a + 1], (128, 128))
        hot_scr[pl.ds(128 * a, 128), :] = jnp.where(column == lanes_all, 1.0, 0.0).astype(BF16)

    for c in range(3):
        q_scr[0, pl.ds(24 * c + 8, 16), :] = jnp.where(
            map_scr[...] > 0, 0.0, nodes_scr[pl.ds(16 * c, 16), :]
        )
    moment_scr[...] = jnp.zeros_like(moment_scr)

    def gather_inner(turn):
        for t in range(4):
            rows_t = row_scr[pl.ds(8 * t, 8), :]
            lanes_t = lane_scr[pl.ds(8 * t, 8), :]
            for c in range(3):
                part_scr[pl.ds(8 * t, 8), 128 * c : 128 * c + 128] = pick(
                    q_scr.at[turn], 24 * c + 8, NODE_ROWS, 8, rows_t, lanes_t, zero
                )

    gather_inner(0)
    send_sum(0, 1, wait_sum(0, 0))

    def moment(index, one, two):
        total = zero
        for c in range(3):
            for t in range(3):
                rows = pl.ds(24 * c + 8 * t, 8)
                total = total + weight_scr[pl.ds(8 * t, 8), :] * q_scr[one, rows, :] * q_scr[two, rows, :]
        moment_scr[pl.ds(index, 1), :] = jnp.sum(total, axis=0, keepdims=True)

    def write_basis(turn):
        for t in range(2):
            where_t = map_scr[pl.ds(8 * t, 8), :]
            rows_t, lanes_t = (where_t >> 6) - 1, where_t & 63
            for c in range(3):
                inner = q_scr[turn, pl.ds(24 * c + 8 + 8 * t, 8), :]
                value = pick(q_scr.at[turn], 24 * c, 8, 0, rows_t, lanes_t, inner)
                for r in range(8 if t == 0 else 4):
                    basis_scr[turn, pl.ds(c, 1), 128 * (8 * t + r) : 128 * (8 * t + r) + 128] = (
                        value[r : r + 1, :]
                    )

    def receive(turn, is_first):
        wait_halo(turn)
        for c in range(3):
            for j in range(PEERS):
                in_scr[pl.ds(8 * c + j, 1), :] = recv_buf[turn, j, c]
        for c in range(3):
            value = own_scr[pl.ds(8 * c, 8), :] + in_scr[pl.ds(8 * c, 8), :]
            if not is_first:
                before = q_scr[turn - 1, pl.ds(24 * c, 8), :]
                scale = spread(scale_scr, 0)
                value = value * scale + before * (DAMPING * scale - 1.0)
            q_scr[turn, pl.ds(24 * c, 8), :] = value

    def stresses(turn):
        for t in range(4):
            rows_t = row_scr[pl.ds(8 * t, 8), :]
            lanes_t = lane_scr[pl.ds(8 * t, 8), :]
            for c in range(3):
                u_scr[pl.ds(8 * t, 8), 128 * c : 128 * c + 128] = pick(
                    q_scr.at[turn],
                    24 * c,
                    8,
                    0,
                    rows_t,
                    lanes_t,
                    part_scr[pl.ds(8 * t, 8), 128 * c : 128 * c + 128],
                )
        high, mid, low = parts_of(u_scr[...])
        right = jnp.concatenate([high, mid, low, high, mid, high], axis=0).astype(BF16)
        g_scr[...] = jnp.dot(first_ref[0:96, :], right, preferred_element_type=F32)
        energy = zero
        for t in range(2):
            grads = [
                g_scr[32 * (n % 3) + 16 * t : 32 * (n % 3) + 16 * t + 16, 128 * (n // 3) : 128 * (n // 3) + 128]
                for n in range(9)
            ]
            for m in range(9):
                total = h_scr[packed_index(m, 0), pl.ds(16 * t, 16), :] * grads[0]
                for n in range(1, 9):
                    total = total + h_scr[packed_index(m, n), pl.ds(16 * t, 16), :] * grads[n]
                product = total * grads[m]
                energy = energy + product[0:8] + product[8:16]
                for p, part in enumerate(parts_of(total)):
                    row = 96 * p + 32 * (m % 3) + 16 * t
                    s_scr[row : row + 16, 128 * (m // 3) : 128 * (m // 3) + 128] = part.astype(BF16)
        return energy

    def terms():
        blocks = jnp.dot(second_ref[...], s_scr[...], preferred_element_type=F32)
        summed = blocks[0:32] + blocks[32:64] + blocks[64:96]
        for p, part in enumerate(parts_of(summed)):
            t_scr[p] = part

    def scatter(target, first, height):
        numbers = lax.broadcasted_iota(jnp.int32, (height, 128), 0) + first
        for a in range(27):
            mask = jnp.broadcast_to(row_scr[pl.ds(a, 1), :], (height, 128)) == numbers
            groups = [
                jnp.where(
                    mask,
                    jnp.broadcast_to(t_scr[p, pl.ds(a, 1), 128 * c : 128 * c + 128], (height, 128)),
                    0.0,
                )
                for c in range(3)
                for p in range(3)
            ]
            if height == 8:
                groups.append(jnp.zeros((8, 128), F32))
                groups = [
                    jnp.concatenate(groups[i : i + 2], axis=0) for i in range(0, len(groups), 2)
                ]
            for i, group in enumerate(groups):
                target[16 * i : 16 * i + 16, 128 * a : 128 * a + 128] = group.astype(BF16)
        summed = jnp.dot(target[...], hot_scr[...], preferred_element_type=F32)
        return [
            summed[3 * height * c : 3 * height * c + height]
            + summed[3 * height * c + height : 3 * height * c + 2 * height]
            + summed[3 * height * c + 2 * height : 3 * height * c + 3 * height]
            for c in range(3)
        ]

    def scatter_shared(turn):
        for c, value in enumerate(scatter(rs_scr, 0, 8)):
            own_scr[pl.ds(8 * c, 8), :] = value
        fill_message(turn + 1)
        send_halo(turn + 1)

    def inner_rows(turn):
        scale = jnp.broadcast_to(scale_scr[0:1, :], (16, 128))
        for c in range(3):
            rows = pl.ds(24 * c + 8, 16)
            q_scr[turn + 1, rows, :] = inner_scr[pl.ds(16 * c, 16), :] * scale + q_scr[
                turn, rows, :
            ] * (DAMPING * scale - 1.0)

    def scatter_inner():
        for c, value in enumerate(scatter(ri_scr, 8, 16)):
            inner_scr[pl.ds(16 * c, 16), :] = value

    def turn_of(turn, is_first):
        receive(turn, is_first)
        stresses(turn)
        terms()
        scatter_shared(turn)
        scatter_inner()
        moment(2 * turn, turn, turn)
        if is_first:
            write_basis(turn)
            row = wait_sum(0, 1)
            total, squares = lane_of(row, 0), lane_of(row, 1)
            scale_scr[0:1, :] = 1.0 / (DAMPING + SHIFT_SCALE * squares / total)
            inner_rows(turn)
            gather_inner(turn + 1)
        else:
            inner_rows(turn)
            gather_inner(turn + 1)
            moment(2 * turn - 1, turn - 1, turn)
            write_basis(turn)

    turn_of(0, True)

    def body(turn, carry):
        turn_of(turn, False)
        return carry

    lax.fori_loop(1, ITERS - 1, body, 0)

    last = ITERS - 1
    receive(last, False)
    moment(2 * last - 1, last - 1, last)
    moment(2 * last, last, last)
    energy = stresses(last)
    moment_scr[pl.ds(2 * last + 1, 1), :] = jnp.sum(energy, axis=0, keepdims=True)
    send_sum(1, 0, row_of(moment_scr[...]))
    terms()
    scatter_shared(last)
    scatter_inner()
    send_sum(1, 1, wait_sum(1, 0))
    inner_rows(last)
    write_basis(last)
    receive(ITERS, False)
    write_basis(ITERS)
    row = wait_sum(1, 1)

    scale = scale_scr[0:1, :]
    m = [lane_of(row, k) for k in range(2 * ITERS)]
    m[2 * last + 1] = m[2 * last + 1] * scale + m[2 * last] * (DAMPING * scale - 1.0)
    low = [[None] * ITERS for _ in range(ITERS)]
    low_d = [[None] * ITERS for _ in range(ITERS)]
    inverse = [None] * ITERS
    right = [None] * ITERS
    for j in range(ITERS):
        pivot = m[2 * j]
        value = m[j + ITERS]
        for k in range(j):
            pivot = pivot - low[j][k] * low_d[j][k]
            value = value - low[j][k] * right[k]
        inverse[j] = 1.0 / pivot
        right[j] = value
        for i in range(j + 1, ITERS):
            entry = m[i + j]
            for k in range(j):
                entry = entry - low[i][k] * low_d[j][k]
            low_d[i][j] = entry
            low[i][j] = entry * inverse[j]
    coef = [None] * ITERS
    for i in reversed(range(ITERS)):
        value = right[i] * inverse[i]
        for k in range(i + 1, ITERS):
            value = value - low[k][i] * coef[k]
        coef[i] = value
    norm = -1.0
    for i in range(ITERS):
        norm = norm - coef[i] if i % 2 == 0 else norm + coef[i]
    by_norm = 1.0 / norm
    rest = [-value * by_norm for value in coef] + [by_norm]
    steps = [1.0 - rest[0]]
    for i in range(1, ITERS):
        steps.append(-rest[i] - steps[-1])
    rest = [jnp.broadcast_to(value, (8, 128)) for value in rest]
    steps = [jnp.broadcast_to(value * scale, (8, 128)) for value in steps]
    for r in range(NODE_ROWS):
        width = min(128, NODES - 128 * r)
        tiles = [basis_scr[i, :, 128 * r : 128 * r + 128] for i in range(ITERS + 1)]
        newton = tiles[0] * steps[0]
        for i in range(1, ITERS):
            newton = newton + tiles[i] * steps[i]
        left = tiles[0] * rest[0]
        for i in range(1, ITERS + 1):
            left = left + tiles[i] * rest[i]
        out_ref[0, :, 128 * r : 128 * r + width] = newton[0:3, 0:width]
        out_ref[1, :, 128 * r : 128 * r + width] = left[0:3, 0:width]

    for turn in range(ITERS + 1):
        pltpu.make_async_copy(send_buf.at[turn], send_buf.at[turn], halo_send.at[turn]).wait()
    for which in range(2):
        for stage in range(2):
            arrived = sum_in[stage].at[which]
            pltpu.make_async_copy(arrived, arrived, sum_send.at[2 * which + stage]).wait()


def shards(count, rhs_partial, connectivity, hessians, shared_nodes, owner):
    first, second = tables()
    sizes = [int(np.prod([d for _, d in digits])) - 1 for digits in stage_digits(count)]
    vmem = pltpu.VMEM
    out = pl.pallas_call(
        functools.partial(kernel, count),
        out_shape=jax.ShapeDtypeStruct((2, 3, NODES), F32),
        in_specs=[pl.BlockSpec(memory_space=vmem)] * 7,
        out_specs=pl.BlockSpec(memory_space=vmem),
        scratch_shapes=[
            vmem((48, 128), F32),
            vmem((16, 128), F32),
            vmem((8, 128), jnp.int32),
            vmem((16, 128), jnp.int32),
            vmem((32, 128), jnp.int32),
            vmem((32, 128), jnp.int32),
            vmem((32, 128), jnp.int32),
            vmem((27 * 128, 128), BF16),
            vmem((45, 32, 128), F32),
            vmem((ITERS + 1, 3 * ROWS, 128), F32),
            vmem((24, 128), F32),
            vmem((48, 128), F32),
            vmem((24, 128), F32),
            vmem((32, 384), F32),
            vmem((32, 384), F32),
            vmem((96, 384), F32),
            vmem((288, 384), BF16),
            vmem((3, 32, 384), F32),
            vmem((80, 27 * 128), BF16),
            vmem((144, 27 * 128), BF16),
            vmem((ROWS, 128), F32),
            vmem((16, 128), F32),
            vmem((8, 128), F32),
            vmem((ITERS + 1, 8, NODE_ROWS * 128), F32),
            vmem((ITERS + 1, PEERS, 3, 1, 128), F32),
            vmem((ITERS + 1, PEERS, 3, 1, 128), F32),
            vmem((4, 1, 128), F32),
            vmem((2, sizes[0], 1, 128), F32),
            vmem((2, sizes[1], 1, 128), F32),
            pltpu.SemaphoreType.DMA((ITERS + 1,)),
            pltpu.SemaphoreType.DMA((ITERS + 1,)),
            pltpu.SemaphoreType.DMA((4,)),
            pltpu.SemaphoreType.DMA((4,)),
        ],
        compiler_params=pltpu.CompilerParams(
            collective_id=0, has_side_effects=True, vmem_limit_bytes=32 * 1024 * 1024
        ),
        name="newton_cg",
    )(
        rhs_partial,
        connectivity,
        hessians,
        shared_nodes,
        owner.reshape(1, NODES),
        jnp.asarray(first),
        jnp.asarray(second),
    )
    return out[0], out[1]


def solution(mesh):
    in_specs = (
        P(None, "parts"),
        P(None, "parts"),
        P(None, None, "parts"),
        P(None, "parts"),
        P("parts"),
    )
    out_specs = (P(None, "parts"), P(None, "parts"))
    return jax.shard_map(
        functools.partial(shards, mesh.shape["parts"]),
        mesh=mesh,
        in_specs=in_specs,
        out_specs=out_specs,
        check_vma=False,
    )
```

```python
import functools

import jax
import jax.numpy as jnp
import ml_dtypes
import numpy as np
from jax import lax
from jax.experimental import pallas as pl
from jax.experimental.pallas import tpu as pltpu
from jax.sharding import PartitionSpec as P

ITERS = 5
DAMPING = 2.0
MESH = pl.DeviceIdType.MESH
F32 = jnp.float32
BF16 = jnp.bfloat16

NODES = 1445
NODE_ROWS = 12
ROWS = 24
PEERS = 8
SHARE = 34
SHIFT_SCALE = 0.045


def shape_table():
    points = np.array([-np.sqrt(0.6), 0.0, np.sqrt(0.6)])
    values = np.stack(
        [points * (points - 1.0) / 2.0, 1.0 - points * points, points * (points + 1.0) / 2.0],
        axis=1,
    )
    slopes = np.stack([points - 0.5, -2.0 * points, points + 0.5], axis=1)
    result = np.zeros((27, 3, 27))
    for direction in range(3):
        factors = [slopes if axis_index == direction else values for axis_index in range(3)]
        product = (
            factors[0][:, None, None, :, None, None]
            * factors[1][None, :, None, None, :, None]
            * factors[2][None, None, :, None, None, :]
        )
        result[:, direction, :] = product.reshape(27, 27)
    return result


def three_parts(table):
    rest = table.astype(np.float32)
    parts = []
    for _ in range(3):
        part = rest.astype(ml_dtypes.bfloat16)
        parts.append(part)
        rest = rest - part.astype(np.float32)
    return parts


def tables():
    table = shape_table()
    forward = np.zeros((3, 32, 32))
    forward[:, :27, :27] = table.transpose(1, 0, 2)
    high, mid, low = three_parts(forward.reshape(96, 32))
    first = np.concatenate([high, high, high, mid, mid, low], axis=1)
    weights = np.einsum("qda,qfa->dfq", table, table)
    row = np.zeros((16, 6, 32))
    for pair, (one, two) in enumerate(PAIRS):
        row[0, pair, :27] = weights[one, two] * (1.0 if one == two else 2.0)
    first = np.concatenate([first, row.reshape(16, 192).astype(ml_dtypes.bfloat16)], axis=0)
    high, mid, low = three_parts(forward.transpose(2, 0, 1).reshape(32, 96))
    zero = np.zeros_like(high)
    second = np.concatenate(
        [
            np.concatenate([high, high, high], axis=1),
            np.concatenate([mid, mid, zero], axis=1),
            np.concatenate([low, zero, zero], axis=1),
        ],
        axis=0,
    )
    return first, second


PAIRS = [(0, 0), (0, 1), (0, 2), (1, 1), (1, 2), (2, 2)]


def packed_index(row_index, col_index):
    first = min(row_index, col_index)
    second = max(row_index, col_index)
    return first * 9 - first * (first - 1) // 2 + (second - first)


def peer_offsets(count):
    half = count // 2
    return [offset - half for offset in range(half)] + [offset + 1 for offset in range(half)]


def stage_digits(count):
    if count == 512:
        return [[(1, 2), (2, 8)], [(16, 8), (128, 4)]]
    small = 1
    while small * small < count:
        small *= 2
    return [[(1, small)], [(small, count // small)]]


def partners(me, digits):
    size = int(np.prod([digit for _, digit in digits]))
    place, scale, base = 0, 1, me
    for stride, digit in digits:
        value = lax.rem(lax.div(me, stride), digit)
        place = place + value * scale
        scale *= digit
        base = base - value * stride
    result = []
    for step in range(1, size):
        other = lax.rem(place + step, size)
        number = base
        for stride, digit in digits:
            number = number + lax.rem(other, digit) * stride
            other = lax.div(other, digit)
        result.append(number)
    return result


def parts_of(value):
    high = value.astype(BF16).astype(F32)
    rest = value - high
    mid = rest.astype(BF16).astype(F32)
    return high, mid, (rest - mid).astype(BF16).astype(F32)


def lane_of(row, lane):
    return jnp.broadcast_to(row[:, lane : lane + 1], (1, 128))


def spread(ref, row):
    return jnp.broadcast_to(ref[pl.ds(row, 1), :], (8, 128))


def pick(ref, base, count, first, rows, lanes, start):
    result = start
    for row in range(count):
        found = jnp.take_along_axis(spread(ref, base + row), lanes, axis=1)
        result = jnp.where(rows == first + row, found, result)
    return result


def kernel(
    count,
    rhs_hbm,
    conn_hbm,
    hess_hbm,
    shared_hbm,
    owner_hbm,
    first_hbm,
    second_hbm,
    out_ref,
    rhs_ref,
    conn_ref,
    hess_ref,
    shared_ref,
    owner_ref,
    first_ref,
    second_ref,
    load_sem,
    nodes_scr,
    owner_scr,
    shared_scr,
    map_scr,
    conn_scr,
    row_scr,
    lane_scr,
    hot_scr,
    wide_scr,
    h_scr,
    q_scr,
    own_scr,
    inner_scr,
    in_scr,
    part_scr,
    u_scr,
    g_scr,
    s_scr,
    t_scr,
    rs_scr,
    ri_scr,
    weight_scr,
    moment_scr,
    scale_scr,
    basis_scr,
    send_buf,
    recv_buf,
    sum_out,
    sum_in0,
    sum_in1,
    halo_send,
    halo_recv,
    sum_send,
    sum_recv,
):
    me = lax.axis_index("parts")
    peers = [lax.rem(me + offset + count, count) for offset in peer_offsets(PEERS)]
    stages = [partners(me, digits) for digits in stage_digits(count)]
    sum_in = [sum_in0, sum_in1]

    barrier = pltpu.get_barrier_semaphore()
    everyone = peers + stages[0] + stages[1]
    for other in everyone:
        pl.semaphore_signal(barrier, inc=1, device_id=(other,), device_id_type=MESH)

    loads = [
        pltpu.make_async_copy(source, target, load_sem.at[i])
        for i, (source, target) in enumerate(
            [
                (rhs_hbm, rhs_ref),
                (shared_hbm, shared_ref),
                (owner_hbm, owner_ref),
                (hess_hbm, hess_ref),
                (first_hbm, first_ref),
                (conn_hbm, conn_ref),
                (second_hbm, second_ref),
            ]
        )
    ]
    for load in loads:
        load.start()

    sublane = lax.broadcasted_iota(jnp.int32, (8, 128), 0)
    lane = lax.broadcasted_iota(jnp.int32, (8, 128), 1)
    sublane16 = lax.broadcasted_iota(jnp.int32, (16, 128), 0)

    def send_halo(turn):
        for j in range(PEERS):
            pltpu.make_async_remote_copy(
                src_ref=send_buf.at[turn, j],
                dst_ref=recv_buf.at[turn, PEERS - 1 - j],
                send_sem=halo_send.at[turn],
                recv_sem=halo_recv.at[turn],
                device_id=(peers[j],),
                device_id_type=MESH,
            ).start()

    def wait_halo(turn):
        pltpu.make_async_copy(recv_buf.at[turn], recv_buf.at[turn], halo_recv.at[turn]).wait()

    def send_sum(which, stage, row):
        slot = 2 * which + stage
        sum_out[slot] = row
        for k, other in enumerate(stages[stage]):
            pltpu.make_async_remote_copy(
                src_ref=sum_out.at[slot],
                dst_ref=sum_in[stage].at[which, k],
                send_sem=sum_send.at[slot],
                recv_sem=sum_recv.at[slot],
                device_id=(other,),
                device_id_type=MESH,
            ).start()

    def wait_sum(which, stage):
        slot = 2 * which + stage
        arrived = sum_in[stage].at[which]
        pltpu.make_async_copy(arrived, arrived, sum_recv.at[slot]).wait()
        terms = [sum_out[slot]] + [sum_in[stage][which, k] for k in range(len(stages[stage]))]
        while len(terms) > 1:
            terms = [sum(terms[i : i + 2]) for i in range(0, len(terms), 2)]
        return terms[0]

    nodes_scr[...] = jnp.zeros_like(nodes_scr)
    owner_scr[...] = jnp.zeros_like(owner_scr)
    for load in loads[0:3]:
        load.wait()
    for r in range(NODE_ROWS):
        width = min(128, NODES - 128 * r)
        for c in range(3):
            nodes_scr[pl.ds(16 * c + r, 1), 0:width] = rhs_ref[c : c + 1, 128 * r : 128 * r + width]
        owner_scr[pl.ds(r, 1), 0:width] = owner_ref[128 * r : 128 * r + width].reshape(1, width).astype(F32)
    shared_scr[...] = jnp.full((8, 128), NODES, jnp.int32)
    shared_scr[:, 0:SHARE] = shared_ref[...]
    names = shared_scr[...]
    used = names < NODES
    name_rows, name_lanes = names >> 7, names & 127
    zero = jnp.zeros((8, 128), F32)
    for c in range(3):
        found = pick(nodes_scr, 16 * c, NODE_ROWS, 0, name_rows, name_lanes, zero)
        own_scr[pl.ds(8 * c, 8), :] = jnp.where(used, found, 0.0)
    weight_scr[0:8, :] = jnp.where(
        used, pick(owner_scr, 0, NODE_ROWS, 0, name_rows, name_lanes, zero), 0.0
    )

    def fill_message(turn):
        for c in range(3):
            for j in range(PEERS):
                send_buf[turn, j, c] = own_scr[pl.ds(8 * c + j, 1), :]

    fill_message(0)
    pl.semaphore_wait(barrier, len(everyone))
    send_halo(0)

    for load in loads[3:]:
        load.wait()
    for q in range(27):
        wide_scr[48 * q : 48 * q + 45, :] = hess_ref[q].astype(F32)
    wide_scr[48 * 27 :, :] = jnp.zeros((48 * 5, 128), F32)
    for k in range(45):
        for t in range(4):
            h_scr[k, 8 * t : 8 * t + 8, :] = wide_scr[pl.ds(48 * 8 * t + k, 8, stride=48), :]
    sums = []
    for one, two in PAIRS:
        total = h_scr[packed_index(one, two)]
        for i in range(1, 3):
            total = total + h_scr[packed_index(3 * i + one, 3 * i + two)]
        sums.append(total)
    stacked = jnp.concatenate(sums, axis=0).astype(BF16)
    traces = jnp.dot(first_ref[96:112, :], stacked, preferred_element_type=F32)[0:1, :]

    def row_of(values):
        totals = jnp.sum(values, axis=1, keepdims=True)
        rows = lax.broadcasted_iota(jnp.int32, values.shape, 0)
        lanes = lax.broadcasted_iota(jnp.int32, values.shape, 1)
        return jnp.sum(jnp.where(rows == lanes, totals, 0.0), axis=0, keepdims=True)

    both = jnp.where(sublane == 0, traces, jnp.where(sublane == 1, traces * traces, 0.0))
    send_sum(0, 0, row_of(both))

    found = jnp.zeros((32, 128), F32)
    for j in range(PEERS):
        rows_j = jnp.broadcast_to(jnp.where(used, name_rows, 99)[j : j + 1, :], (16, 128))
        lanes_j = jnp.broadcast_to(name_lanes[j : j + 1, :], (128, 128))
        hit = rows_j == sublane16
        slot = lax.broadcasted_iota(jnp.int32, (16, 128), 1).astype(F32)
        left = jnp.concatenate(
            [jnp.where(hit, float(j + 1), 0.0), jnp.where(hit, slot, 0.0)], axis=0
        )
        right = jnp.where(
            lanes_j == lax.broadcasted_iota(jnp.int32, (128, 128), 0), 1.0, 0.0
        )
        found = found + lax.dot_general(
            left.astype(BF16),
            right.astype(BF16),
            (((1,), (1,)), ((), ())),
            preferred_element_type=F32,
        )
    map_scr[...] = (64.0 * found[0:16] + found[16:32]).astype(jnp.int32)
    weight_scr[8:24, :] = jnp.where(map_scr[...] > 0, 0.0, owner_scr[...])

    conn_scr[...] = jnp.zeros_like(conn_scr)
    conn_scr[0:27, :] = conn_ref[...]
    for t in range(4):
        names_t = conn_scr[pl.ds(8 * t, 8), :]
        rows_t, lanes_t = names_t >> 7, names_t & 127
        where_t = pick(map_scr, 0, NODE_ROWS, 0, rows_t, lanes_t, jnp.zeros((8, 128), jnp.int32))
        is_shared = where_t > 0
        row_t = jnp.where(is_shared, (where_t >> 6) - 1, rows_t + 8)
        if t == 3:
            row_t = jnp.where(sublane < 3, row_t, 99)
        row_scr[pl.ds(8 * t, 8), :] = row_t
        lane_scr[pl.ds(8 * t, 8), :] = jnp.where(is_shared, where_t & 63, lanes_t)

    columns = jnp.transpose(lane_scr[...].astype(F32))
    lanes_all = lax.broadcasted_iota(jnp.int32, (128, 128), 1).astype(F32)
    for a in range(27):
        column = jnp.broadcast_to(columns[:, a : a + 1], (128, 128))
        hot_scr[pl.ds(128 * a, 128), :] = jnp.where(column == lanes_all, 1.0, 0.0).astype(BF16)

    for c in range(3):
        q_scr[0, pl.ds(24 * c + 8, 16), :] = jnp.where(
            map_scr[...] > 0, 0.0, nodes_scr[pl.ds(16 * c, 16), :]
        )
    moment_scr[...] = jnp.zeros_like(moment_scr)

    def gather_inner(turn):
        for t in range(4):
            rows_t = row_scr[pl.ds(8 * t, 8), :]
            lanes_t = lane_scr[pl.ds(8 * t, 8), :]
            for c in range(3):
                part_scr[pl.ds(8 * t, 8), 128 * c : 128 * c + 128] = pick(
                    q_scr.at[turn], 24 * c + 8, NODE_ROWS, 8, rows_t, lanes_t, zero
                )

    gather_inner(0)
    send_sum(0, 1, wait_sum(0, 0))

    def moment(index, one, two):
        total = zero
        for c in range(3):
            for t in range(3):
                rows = pl.ds(24 * c + 8 * t, 8)
                total = total + weight_scr[pl.ds(8 * t, 8), :] * q_scr[one, rows, :] * q_scr[two, rows, :]
        moment_scr[pl.ds(index, 1), :] = jnp.sum(total, axis=0, keepdims=True)

    def write_basis(turn):
        for t in range(2):
            where_t = map_scr[pl.ds(8 * t, 8), :]
            rows_t, lanes_t = (where_t >> 6) - 1, where_t & 63
            for c in range(3):
                inner = q_scr[turn, pl.ds(24 * c + 8 + 8 * t, 8), :]
                value = pick(q_scr.at[turn], 24 * c, 8, 0, rows_t, lanes_t, inner)
                for r in range(8 if t == 0 else 4):
                    basis_scr[turn, pl.ds(c, 1), 128 * (8 * t + r) : 128 * (8 * t + r) + 128] = (
                        value[r : r + 1, :]
                    )

    def receive(turn, is_first):
        wait_halo(turn)
        for c in range(3):
            for j in range(PEERS):
                in_scr[pl.ds(8 * c + j, 1), :] = recv_buf[turn, j, c]
        for c in range(3):
            value = own_scr[pl.ds(8 * c, 8), :] + in_scr[pl.ds(8 * c, 8), :]
            if not is_first:
                before = q_scr[turn - 1, pl.ds(24 * c, 8), :]
                scale = spread(scale_scr, 0)
                value = value * scale + before * (DAMPING * scale - 1.0)
            q_scr[turn, pl.ds(24 * c, 8), :] = value

    def stresses(turn):
        for t in range(4):
            rows_t = row_scr[pl.ds(8 * t, 8), :]
            lanes_t = lane_scr[pl.ds(8 * t, 8), :]
            for c in range(3):
                u_scr[pl.ds(8 * t, 8), 128 * c : 128 * c + 128] = pick(
                    q_scr.at[turn],
                    24 * c,
                    8,
                    0,
                    rows_t,
                    lanes_t,
                    part_scr[pl.ds(8 * t, 8), 128 * c : 128 * c + 128],
                )
        high, mid, low = parts_of(u_scr[...])
        right = jnp.concatenate([high, mid, low, high, mid, high], axis=0).astype(BF16)
        g_scr[...] = jnp.dot(first_ref[0:96, :], right, preferred_element_type=F32)
        energy = zero
        for t in range(2):
            grads = [
                g_scr[32 * (n % 3) + 16 * t : 32 * (n % 3) + 16 * t + 16, 128 * (n // 3) : 128 * (n // 3) + 128]
                for n in range(9)
            ]
            for m in range(9):
                total = h_scr[packed_index(m, 0), pl.ds(16 * t, 16), :] * grads[0]
                for n in range(1, 9):
                    total = total + h_scr[packed_index(m, n), pl.ds(16 * t, 16), :] * grads[n]
                product = total * grads[m]
                energy = energy + product[0:8] + product[8:16]
                for p, part in enumerate(parts_of(total)):
                    row = 96 * p + 32 * (m % 3) + 16 * t
                    s_scr[row : row + 16, 128 * (m // 3) : 128 * (m // 3) + 128] = part.astype(BF16)
        return energy

    def terms():
        blocks = jnp.dot(second_ref[...], s_scr[...], preferred_element_type=F32)
        summed = blocks[0:32] + blocks[32:64] + blocks[64:96]
        for p, part in enumerate(parts_of(summed)):
            t_scr[p] = part

    def scatter(target, first, height):
        numbers = lax.broadcasted_iota(jnp.int32, (height, 128), 0) + first
        for a in range(27):
            mask = jnp.broadcast_to(row_scr[pl.ds(a, 1), :], (height, 128)) == numbers
            groups = [
                jnp.where(
                    mask,
                    jnp.broadcast_to(t_scr[p, pl.ds(a, 1), 128 * c : 128 * c + 128], (height, 128)),
                    0.0,
                )
                for c in range(3)
                for p in range(3)
            ]
            if height == 8:
                groups.append(jnp.zeros((8, 128), F32))
                groups = [
                    jnp.concatenate(groups[i : i + 2], axis=0) for i in range(0, len(groups), 2)
                ]
            for i, group in enumerate(groups):
                target[16 * i : 16 * i + 16, 128 * a : 128 * a + 128] = group.astype(BF16)
        summed = jnp.dot(target[...], hot_scr[...], preferred_element_type=F32)
        return [
            summed[3 * height * c : 3 * height * c + height]
            + summed[3 * height * c + height : 3 * height * c + 2 * height]
            + summed[3 * height * c + 2 * height : 3 * height * c + 3 * height]
            for c in range(3)
        ]

    def scatter_shared(turn):
        for c, value in enumerate(scatter(rs_scr, 0, 8)):
            own_scr[pl.ds(8 * c, 8), :] = value
        fill_message(turn + 1)
        send_halo(turn + 1)

    def inner_rows(turn):
        scale = jnp.broadcast_to(scale_scr[0:1, :], (16, 128))
        for c in range(3):
            rows = pl.ds(24 * c + 8, 16)
            q_scr[turn + 1, rows, :] = inner_scr[pl.ds(16 * c, 16), :] * scale + q_scr[
                turn, rows, :
            ] * (DAMPING * scale - 1.0)

    def scatter_inner():
        for c, value in enumerate(scatter(ri_scr, 8, 16)):
            inner_scr[pl.ds(16 * c, 16), :] = value

    def turn_of(turn, is_first):
        receive(turn, is_first)
        stresses(turn)
        terms()
        scatter_shared(turn)
        scatter_inner()
        moment(2 * turn, turn, turn)
        if is_first:
            write_basis(turn)
            row = wait_sum(0, 1)
            total, squares = lane_of(row, 0), lane_of(row, 1)
            scale_scr[0:1, :] = 1.0 / (DAMPING + SHIFT_SCALE * squares / total)
            inner_rows(turn)
            gather_inner(turn + 1)
        else:
            inner_rows(turn)
            gather_inner(turn + 1)
            moment(2 * turn - 1, turn - 1, turn)
            write_basis(turn)

    turn_of(0, True)

    def body(turn, carry):
        turn_of(turn, False)
        return carry

    lax.fori_loop(1, ITERS - 1, body, 0)

    last = ITERS - 1
    receive(last, False)
    moment(2 * last - 1, last - 1, last)
    moment(2 * last, last, last)
    energy = stresses(last)
    moment_scr[pl.ds(2 * last + 1, 1), :] = jnp.sum(energy, axis=0, keepdims=True)
    send_sum(1, 0, row_of(moment_scr[...]))
    terms()
    scatter_shared(last)
    scatter_inner()
    send_sum(1, 1, wait_sum(1, 0))
    inner_rows(last)
    write_basis(last)
    receive(ITERS, False)
    write_basis(ITERS)
    row = wait_sum(1, 1)

    scale = scale_scr[0:1, :]
    m = [lane_of(row, k) for k in range(2 * ITERS)]
    m[2 * last + 1] = m[2 * last + 1] * scale + m[2 * last] * (DAMPING * scale - 1.0)
    low = [[None] * ITERS for _ in range(ITERS)]
    low_d = [[None] * ITERS for _ in range(ITERS)]
    inverse = [None] * ITERS
    right = [None] * ITERS
    for j in range(ITERS):
        pivot = m[2 * j]
        value = m[j + ITERS]
        for k in range(j):
            pivot = pivot - low[j][k] * low_d[j][k]
            value = value - low[j][k] * right[k]
        inverse[j] = 1.0 / pivot
        right[j] = value
        for i in range(j + 1, ITERS):
            entry = m[i + j]
            for k in range(j):
                entry = entry - low[i][k] * low_d[j][k]
            low_d[i][j] = entry
            low[i][j] = entry * inverse[j]
    coef = [None] * ITERS
    for i in reversed(range(ITERS)):
        value = right[i] * inverse[i]
        for k in range(i + 1, ITERS):
            value = value - low[k][i] * coef[k]
        coef[i] = value
    norm = -1.0
    for i in range(ITERS):
        norm = norm - coef[i] if i % 2 == 0 else norm + coef[i]
    by_norm = 1.0 / norm
    rest = [-value * by_norm for value in coef] + [by_norm]
    steps = [1.0 - rest[0]]
    for i in range(1, ITERS):
        steps.append(-rest[i] - steps[-1])
    rest = [jnp.broadcast_to(value, (8, 128)) for value in rest]
    steps = [jnp.broadcast_to(value * scale, (8, 128)) for value in steps]
    for r in range(NODE_ROWS):
        width = min(128, NODES - 128 * r)
        tiles = [basis_scr[i, :, 128 * r : 128 * r + 128] for i in range(ITERS + 1)]
        newton = tiles[0] * steps[0]
        for i in range(1, ITERS):
            newton = newton + tiles[i] * steps[i]
        left = tiles[0] * rest[0]
        for i in range(1, ITERS + 1):
            left = left + tiles[i] * rest[i]
        out_ref[0, :, 128 * r : 128 * r + width] = newton[0:3, 0:width]
        out_ref[1, :, 128 * r : 128 * r + width] = left[0:3, 0:width]

    for turn in range(ITERS + 1):
        pltpu.make_async_copy(send_buf.at[turn], send_buf.at[turn], halo_send.at[turn]).wait()
    for which in range(2):
        for stage in range(2):
            arrived = sum_in[stage].at[which]
            pltpu.make_async_copy(arrived, arrived, sum_send.at[2 * which + stage]).wait()


def shards(count, rhs_partial, connectivity, hessians, shared_nodes, owner):
    first, second = tables()
    sizes = [int(np.prod([d for _, d in digits])) - 1 for digits in stage_digits(count)]
    vmem = pltpu.VMEM
    out = pl.pallas_call(
        functools.partial(kernel, count),
        out_shape=vmem((2, 3, NODES), F32),
        in_specs=[pl.BlockSpec(memory_space=pltpu.HBM)] * 7,
        out_specs=pl.BlockSpec(memory_space=vmem),
        scratch_shapes=[
            vmem((3, NODES), F32),
            vmem((27, 128), jnp.int32),
            vmem((27, 45, 128), BF16),
            vmem((8, SHARE), jnp.int32),
            vmem((NODES,), jnp.int32),
            vmem(first.shape, BF16),
            vmem(second.shape, BF16),
            pltpu.SemaphoreType.DMA((7,)),
            vmem((48, 128), F32),
            vmem((16, 128), F32),
            vmem((8, 128), jnp.int32),
            vmem((16, 128), jnp.int32),
            vmem((32, 128), jnp.int32),
            vmem((32, 128), jnp.int32),
            vmem((32, 128), jnp.int32),
            vmem((27 * 128, 128), BF16),
            vmem((48 * 32, 128), F32),
            vmem((45, 32, 128), F32),
            vmem((ITERS + 1, 3 * ROWS, 128), F32),
            vmem((24, 128), F32),
            vmem((48, 128), F32),
            vmem((24, 128), F32),
            vmem((32, 384), F32),
            vmem((32, 384), F32),
            vmem((96, 384), F32),
            vmem((288, 384), BF16),
            vmem((3, 32, 384), F32),
            vmem((80, 27 * 128), BF16),
            vmem((144, 27 * 128), BF16),
            vmem((ROWS, 128), F32),
            vmem((16, 128), F32),
            vmem((8, 128), F32),
            vmem((ITERS + 1, 8, NODE_ROWS * 128), F32),
            vmem((ITERS + 1, PEERS, 3, 1, 128), F32),
            vmem((ITERS + 1, PEERS, 3, 1, 128), F32),
            vmem((4, 1, 128), F32),
            vmem((2, sizes[0], 1, 128), F32),
            vmem((2, sizes[1], 1, 128), F32),
            pltpu.SemaphoreType.DMA((ITERS + 1,)),
            pltpu.SemaphoreType.DMA((ITERS + 1,)),
            pltpu.SemaphoreType.DMA((4,)),
            pltpu.SemaphoreType.DMA((4,)),
        ],
        compiler_params=pltpu.CompilerParams(collective_id=0, has_side_effects=True),
        name="newton_cg",
    )(
        rhs_partial,
        connectivity,
        jnp.transpose(hessians, (1, 0, 2)),
        shared_nodes,
        owner,
        jnp.asarray(first),
        jnp.asarray(second),
    )
    return out[0], out[1]


def solution(mesh):
    in_specs = (
        P(None, "parts"),
        P(None, "parts"),
        P(None, None, "parts"),
        P(None, "parts"),
        P("parts"),
    )
    out_specs = (P(None, "parts"), P(None, "parts"))
    return jax.shard_map(
        functools.partial(shards, mesh.shape["parts"]),
        mesh=mesh,
        in_specs=in_specs,
        out_specs=out_specs,
        check_vma=False,
    )
```

```python
import functools

import jax
import jax.numpy as jnp
import ml_dtypes
import numpy as np
from jax import lax
from jax.experimental import pallas as pl
from jax.experimental.pallas import tpu as pltpu
from jax.sharding import PartitionSpec as P

ITERS = 5
DAMPING = 2.0
MESH = pl.DeviceIdType.MESH
F32 = jnp.float32
BF16 = jnp.bfloat16

NODES = 1445
NODE_ROWS = 12
BASE = 4
ROWS = BASE + NODE_ROWS
PEERS = 8
SHARE = 34
PEER_ROW = [0, 0, 0, 2, 3, 1, 1, 1]
PEER_LANE = [0, 40, 80, 0, 0, 80, 40, 0]
SHIFT_SCALE = 0.045


def shape_table():
    points = np.array([-np.sqrt(0.6), 0.0, np.sqrt(0.6)])
    values = np.stack(
        [points * (points - 1.0) / 2.0, 1.0 - points * points, points * (points + 1.0) / 2.0],
        axis=1,
    )
    slopes = np.stack([points - 0.5, -2.0 * points, points + 0.5], axis=1)
    result = np.zeros((27, 3, 27))
    for direction in range(3):
        factors = [slopes if axis_index == direction else values for axis_index in range(3)]
        product = (
            factors[0][:, None, None, :, None, None]
            * factors[1][None, :, None, None, :, None]
            * factors[2][None, None, :, None, None, :]
        )
        result[:, direction, :] = product.reshape(27, 27)
    return result


def three_parts(table):
    rest = table.astype(np.float32)
    parts = []
    for _ in range(3):
        part = rest.astype(ml_dtypes.bfloat16)
        parts.append(part)
        rest = rest - part.astype(np.float32)
    return parts


def tables():
    table = shape_table()
    forward = np.zeros((3, 32, 32))
    forward[:, :27, :27] = table.transpose(1, 0, 2)
    high, mid, low = three_parts(forward.reshape(96, 32))
    first = np.concatenate([high, high, high, mid, mid, low], axis=1)
    weights = np.einsum("qda,qfa->dfq", table, table)
    row = np.zeros((16, 6, 32))
    for pair, (one, two) in enumerate(PAIRS):
        row[0, pair, :27] = weights[one, two] * (1.0 if one == two else 2.0)
    first = np.concatenate([first, row.reshape(16, 192).astype(ml_dtypes.bfloat16)], axis=0)
    high, mid, low = three_parts(forward.transpose(2, 0, 1).reshape(32, 96))
    zero = np.zeros_like(high)
    second = np.concatenate(
        [
            np.concatenate([high, high, high], axis=1),
            np.concatenate([mid, mid, zero], axis=1),
            np.concatenate([low, zero, zero], axis=1),
        ],
        axis=0,
    )
    return first, second


PAIRS = [(0, 0), (0, 1), (0, 2), (1, 1), (1, 2), (2, 2)]


def packed_index(row_index, col_index):
    first = min(row_index, col_index)
    second = max(row_index, col_index)
    return first * 9 - first * (first - 1) // 2 + (second - first)


def peer_offsets(count):
    half = count // 2
    return [offset - half for offset in range(half)] + [offset + 1 for offset in range(half)]


def stage_masks(count):
    bits = count.bit_length() - 1
    low = 1 << min(4, bits - 1)
    return [list(range(1, low)), [low * k for k in range(1, count // low)]]


def parts_of(value):
    high = value.astype(BF16).astype(F32)
    rest = value - high
    mid = rest.astype(BF16).astype(F32)
    return high, mid, (rest - mid).astype(BF16).astype(F32)


def lane_of(row, lane):
    return jnp.broadcast_to(row[:, lane : lane + 1], (1, 128))


def spread(ref, row):
    return jnp.broadcast_to(ref[pl.ds(row, 1), :], (8, 128))


def pick(ref, base, count, first, rows, lanes, start):
    result = start
    for row in range(count):
        found = jnp.take_along_axis(spread(ref, base + row), lanes, axis=1)
        result = jnp.where(rows == first + row, found, result)
    return result


def kernel(
    count,
    rhs_hbm,
    conn_hbm,
    hess_hbm,
    shared_hbm,
    owner_hbm,
    first_hbm,
    second_hbm,
    out_ref,
    rhs_ref,
    conn_ref,
    hess_ref,
    shared_ref,
    owner_ref,
    first_ref,
    second_ref,
    load_sem,
    nodes_scr,
    owner_scr,
    shared_scr,
    map_scr,
    conn_scr,
    row_scr,
    lane_scr,
    hot_scr,
    wide_scr,
    h_scr,
    q_scr,
    own_scr,
    inner_scr,
    in_scr,
    part_scr,
    u_scr,
    g_scr,
    s_scr,
    t_scr,
    weight_scr,
    moment_scr,
    scale_scr,
    basis_scr,
    send_buf,
    recv_buf,
    sum_out,
    sum_in0,
    sum_in1,
    halo_send,
    halo_recv,
    sum_send,
    sum_recv,
):
    me = lax.axis_index("parts")
    peers = [(me + offset) & (count - 1) for offset in peer_offsets(PEERS)]
    stages = [[me ^ mask for mask in masks] for masks in stage_masks(count)]
    sum_in = [sum_in0, sum_in1]

    barrier = pltpu.get_barrier_semaphore()
    everyone = peers + stages[0] + stages[1]
    for other in everyone:
        pl.semaphore_signal(barrier, inc=1, device_id=(other,), device_id_type=MESH)

    loads = [
        pltpu.make_async_copy(source, target, load_sem.at[i])
        for i, (source, target) in enumerate(
            [
                (rhs_hbm, rhs_ref),
                (shared_hbm, shared_ref),
                (owner_hbm, owner_ref),
                (hess_hbm, hess_ref),
                (first_hbm, first_ref),
                (conn_hbm, conn_ref),
                (second_hbm, second_ref),
            ]
        )
    ]
    for load in loads:
        load.start()

    sublane = lax.broadcasted_iota(jnp.int32, (8, 128), 0)
    lane = lax.broadcasted_iota(jnp.int32, (8, 128), 1)
    sublane16 = lax.broadcasted_iota(jnp.int32, (16, 128), 0)

    def send_halo(turn):
        for j in range(PEERS):
            pltpu.make_async_remote_copy(
                src_ref=send_buf.at[turn, PEER_ROW[j]],
                dst_ref=recv_buf.at[turn, PEERS - 1 - j],
                send_sem=halo_send.at[turn],
                recv_sem=halo_recv.at[turn],
                device_id=(peers[j],),
                device_id_type=MESH,
            ).start()

    def wait_halo(turn):
        pltpu.make_async_copy(recv_buf.at[turn], recv_buf.at[turn], halo_recv.at[turn]).wait()

    def send_sum(which, stage, row):
        slot = 2 * which + stage
        sum_out[slot] = row
        for k, other in enumerate(stages[stage]):
            pltpu.make_async_remote_copy(
                src_ref=sum_out.at[slot],
                dst_ref=sum_in[stage].at[which, k],
                send_sem=sum_send.at[slot],
                recv_sem=sum_recv.at[slot],
                device_id=(other,),
                device_id_type=MESH,
            ).start()

    def wait_sum(which, stage):
        slot = 2 * which + stage
        arrived = sum_in[stage].at[which]
        pltpu.make_async_copy(arrived, arrived, sum_recv.at[slot]).wait()
        terms = [sum_out[slot]] + [sum_in[stage][which, k] for k in range(len(stages[stage]))]
        while len(terms) > 1:
            terms = [sum(terms[i : i + 2]) for i in range(0, len(terms), 2)]
        return terms[0]

    nodes_scr[...] = jnp.zeros_like(nodes_scr)
    owner_scr[...] = jnp.zeros_like(owner_scr)
    for load in loads[0:3]:
        load.wait()
    for r in range(NODE_ROWS):
        width = min(128, NODES - 128 * r)
        for c in range(3):
            nodes_scr[pl.ds(16 * c + BASE + r, 1), 0:width] = rhs_ref[c : c + 1, 128 * r : 128 * r + width]
        owner_scr[pl.ds(BASE + r, 1), 0:width] = owner_ref[128 * r : 128 * r + width].reshape(1, width).astype(F32)
    shared_scr[...] = jnp.full((8, 128), NODES, jnp.int32)
    for j in range(PEERS):
        start = PEER_LANE[j]
        shared_scr[PEER_ROW[j] : PEER_ROW[j] + 1, start : start + SHARE] = shared_ref[j : j + 1, :]
    names = shared_scr[...]
    used = names < NODES
    name_rows, name_lanes = (names >> 7) + BASE, names & 127
    zero = jnp.zeros((8, 128), F32)
    for c in range(3):
        found = pick(nodes_scr, 16 * c + BASE, NODE_ROWS, BASE, name_rows, name_lanes, zero)
        own_scr[pl.ds(8 * c, 8), :] = jnp.where(used, found, 0.0)
    owned = pick(owner_scr, BASE, NODE_ROWS, BASE, name_rows, name_lanes, zero)
    shared_weight = jnp.where(used, owned, 0.0)

    def fill_message(turn):
        for c in range(3):
            for row in range(BASE):
                send_buf[turn, row, c] = own_scr[pl.ds(8 * c + row, 1), :]

    fill_message(0)
    pl.semaphore_wait(barrier, len(everyone))
    send_halo(0)

    for load in loads[3:]:
        load.wait()
    for q in range(27):
        wide_scr[48 * q : 48 * q + 45, :] = hess_ref[q].astype(F32)
    wide_scr[48 * 27 :, :] = jnp.zeros((48 * 5, 128), F32)
    for k in range(45):
        for t in range(4):
            h_scr[k, 8 * t : 8 * t + 8, :] = wide_scr[pl.ds(48 * 8 * t + k, 8, stride=48), :]
    sums = []
    for one, two in PAIRS:
        total = h_scr[packed_index(one, two)]
        for i in range(1, 3):
            total = total + h_scr[packed_index(3 * i + one, 3 * i + two)]
        sums.append(total)
    stacked = jnp.concatenate(sums, axis=0).astype(BF16)
    traces = jnp.dot(first_ref[96:112, :], stacked, preferred_element_type=F32)[0:1, :]

    def row_of(values):
        totals = jnp.sum(values, axis=1, keepdims=True)
        rows = lax.broadcasted_iota(jnp.int32, values.shape, 0)
        lanes = lax.broadcasted_iota(jnp.int32, values.shape, 1)
        return jnp.sum(jnp.where(rows == lanes, totals, 0.0), axis=0, keepdims=True)

    both = jnp.where(sublane == 0, traces, jnp.where(sublane == 1, traces * traces, 0.0))
    send_sum(0, 0, row_of(both))

    found = jnp.zeros((32, 128), F32)
    for j in range(BASE):
        rows_j = jnp.broadcast_to(jnp.where(used, name_rows, 99)[j : j + 1, :], (16, 128))
        lanes_j = jnp.broadcast_to(name_lanes[j : j + 1, :], (128, 128))
        hit = rows_j == sublane16
        slot = lax.broadcasted_iota(jnp.int32, (16, 128), 1).astype(F32)
        left = jnp.concatenate(
            [jnp.where(hit, float(j + 1), 0.0), jnp.where(hit, slot, 0.0)], axis=0
        )
        right = jnp.where(
            lanes_j == lax.broadcasted_iota(jnp.int32, (128, 128), 0), 1.0, 0.0
        )
        found = found + lax.dot_general(
            left.astype(BF16),
            right.astype(BF16),
            (((1,), (1,)), ((), ())),
            preferred_element_type=F32,
        )
    map_scr[...] = (128.0 * found[0:16] + found[16:32]).astype(jnp.int32)
    others = jnp.where(map_scr[...] > 0, 0.0, owner_scr[...])
    weight_scr[0:8, :] = others[0:8] + shared_weight
    weight_scr[8:16, :] = others[8:16]

    conn_scr[...] = jnp.zeros_like(conn_scr)
    conn_scr[0:27, :] = conn_ref[...]
    for t in range(4):
        names_t = conn_scr[pl.ds(8 * t, 8), :]
        rows_t, lanes_t = (names_t >> 7) + BASE, names_t & 127
        where_t = pick(map_scr, BASE, NODE_ROWS, BASE, rows_t, lanes_t, jnp.zeros((8, 128), jnp.int32))
        is_shared = where_t > 0
        row_t = jnp.where(is_shared, (where_t >> 7) - 1, rows_t)
        if t == 3:
            row_t = jnp.where(sublane < 3, row_t, 99)
        row_scr[pl.ds(8 * t, 8), :] = row_t
        lane_scr[pl.ds(8 * t, 8), :] = jnp.where(is_shared, where_t & 127, lanes_t)

    columns = jnp.transpose(lane_scr[...].astype(F32))
    lanes_all = lax.broadcasted_iota(jnp.int32, (128, 128), 1).astype(F32)
    for a in range(27):
        column = jnp.broadcast_to(columns[:, a : a + 1], (128, 128))
        hot_scr[pl.ds(128 * a, 128), :] = jnp.where(column == lanes_all, 1.0, 0.0).astype(BF16)

    for c in range(3):
        q_scr[0, pl.ds(16 * c, 16), :] = jnp.where(
            map_scr[...] > 0, 0.0, nodes_scr[pl.ds(16 * c, 16), :]
        )
    moment_scr[...] = jnp.zeros_like(moment_scr)

    def gather_inner(turn):
        for t in range(4):
            rows_t = row_scr[pl.ds(8 * t, 8), :]
            lanes_t = lane_scr[pl.ds(8 * t, 8), :]
            for c in range(3):
                part_scr[pl.ds(8 * t, 8), 128 * c : 128 * c + 128] = pick(
                    q_scr.at[turn], 16 * c + BASE, NODE_ROWS, BASE, rows_t, lanes_t, zero
                )

    gather_inner(0)
    send_sum(0, 1, wait_sum(0, 0))

    def moment(index, one, two):
        total = zero
        for c in range(3):
            for t in range(2):
                rows = pl.ds(16 * c + 8 * t, 8)
                total = total + weight_scr[pl.ds(8 * t, 8), :] * q_scr[one, rows, :] * q_scr[two, rows, :]
        moment_scr[pl.ds(index, 1), :] = jnp.sum(total, axis=0, keepdims=True)

    def write_basis(turn):
        for t in range(2):
            where_t = map_scr[pl.ds(8 * t, 8), :]
            rows_t, lanes_t = (where_t >> 7) - 1, where_t & 127
            for c in range(3):
                inner = q_scr[turn, pl.ds(16 * c + 8 * t, 8), :]
                value = pick(q_scr.at[turn], 16 * c, BASE, 0, rows_t, lanes_t, inner)
                for row in range(BASE if t == 0 else 0, 8):
                    start = 128 * (8 * t + row - BASE)
                    basis_scr[turn, pl.ds(c, 1), start : start + 128] = value[row : row + 1, :]

    def receive(turn, is_first):
        wait_halo(turn)
        lanes = lax.broadcasted_iota(jnp.int32, (1, 128), 1)
        for c in range(3):
            arrived = [recv_buf[turn, j, c] for j in range(PEERS)]
            for row in range(BASE):
                own = [j for j in range(PEERS) if PEER_ROW[j] == row]
                own.sort(key=lambda j: PEER_LANE[j])
                value = arrived[own[0]]
                for j in own[1:]:
                    value = jnp.where(lanes >= PEER_LANE[j], arrived[j], value)
                in_scr[pl.ds(8 * c + row, 1), :] = value
        for c in range(3):
            value = own_scr[pl.ds(8 * c, BASE), :] + in_scr[pl.ds(8 * c, BASE), :]
            if not is_first:
                before = q_scr[turn - 1, pl.ds(16 * c, BASE), :]
                scale = jnp.broadcast_to(scale_scr[0:1, :], (BASE, 128))
                value = value * scale + before * (DAMPING * scale - 1.0)
            q_scr[turn, pl.ds(16 * c, BASE), :] = value

    def stresses(turn):
        for t in range(4):
            rows_t = row_scr[pl.ds(8 * t, 8), :]
            lanes_t = lane_scr[pl.ds(8 * t, 8), :]
            for c in range(3):
                u_scr[pl.ds(8 * t, 8), 128 * c : 128 * c + 128] = pick(
                    q_scr.at[turn],
                    16 * c,
                    BASE,
                    0,
                    rows_t,
                    lanes_t,
                    part_scr[pl.ds(8 * t, 8), 128 * c : 128 * c + 128],
                )
        high, mid, low = parts_of(u_scr[...])
        right = jnp.concatenate([high, mid, low, high, mid, high], axis=0).astype(BF16)
        g_scr[...] = jnp.dot(first_ref[0:96, :], right, preferred_element_type=F32)
        energy = zero
        for t in range(2):
            grads = [
                g_scr[32 * (n % 3) + 16 * t : 32 * (n % 3) + 16 * t + 16, 128 * (n // 3) : 128 * (n // 3) + 128]
                for n in range(9)
            ]
            for m in range(9):
                total = h_scr[packed_index(m, 0), pl.ds(16 * t, 16), :] * grads[0]
                for n in range(1, 9):
                    total = total + h_scr[packed_index(m, n), pl.ds(16 * t, 16), :] * grads[n]
                product = total * grads[m]
                energy = energy + product[0:8] + product[8:16]
                for p, part in enumerate(parts_of(total)):
                    row = 96 * p + 32 * (m % 3) + 16 * t
                    s_scr[row : row + 16, 128 * (m // 3) : 128 * (m // 3) + 128] = part.astype(BF16)
        return energy

    def terms():
        blocks = jnp.dot(second_ref[...], s_scr[...], preferred_element_type=F32)
        summed = blocks[0:32] + blocks[32:64] + blocks[64:96]
        for p, part in enumerate(parts_of(summed)):
            t_scr[p] = part

    def term(p, a, c, height):
        row = t_scr[p, pl.ds(a, 1), 128 * c : 128 * c + 128]
        return jnp.broadcast_to(row, (height, 128))

    def by_lane(left):
        summed = None
        for a in range(0, 27, 4):
            part = jnp.dot(
                jnp.concatenate(left[a : a + 4], axis=1),
                hot_scr[128 * a : 128 * min(a + 4, 27), :],
                preferred_element_type=F32,
            )
            summed = part if summed is None else summed + part
        return summed

    def scatter_shared(turn):
        order = [(c, p) for c in range(3) for p in range(3)]
        upper = sublane < BASE
        numbers = sublane & (BASE - 1)
        left = []
        for a in range(27):
            mask = spread(row_scr, a) == numbers
            tiles = []
            for i in range(0, 9, 2):
                value = term(order[i][1], a, order[i][0], 8)
                if i < 8:
                    other = term(order[i + 1][1], a, order[i + 1][0], 8)
                    tiles.append(jnp.where(mask, jnp.where(upper, value, other), 0.0))
                else:
                    tiles.append(jnp.where(mask & upper, value, 0.0))
            tiles.append(zero)
            left.append(jnp.concatenate(tiles, axis=0).astype(BF16))
        summed = by_lane(left)
        for c in range(3):
            own_scr[pl.ds(8 * c, BASE), :] = (
                summed[12 * c : 12 * c + 4]
                + summed[12 * c + 4 : 12 * c + 8]
                + summed[12 * c + 8 : 12 * c + 12]
            )
        fill_message(turn + 1)
        send_halo(turn + 1)

    def scatter_inner():
        left = []
        for a in range(27):
            mask = jnp.broadcast_to(row_scr[pl.ds(a, 1), :], (16, 128)) == sublane16
            tiles = [jnp.where(mask, term(p, a, c, 16), 0.0) for c in range(3) for p in range(3)]
            left.append(jnp.concatenate(tiles, axis=0).astype(BF16))
        summed = by_lane(left)
        for c in range(3):
            inner_scr[pl.ds(16 * c, 16), :] = (
                summed[48 * c : 48 * c + 16]
                + summed[48 * c + 16 : 48 * c + 32]
                + summed[48 * c + 32 : 48 * c + 48]
            )

    def inner_rows(turn):
        scale = jnp.broadcast_to(scale_scr[0:1, :], (16, 128))
        for c in range(3):
            rows = pl.ds(16 * c, 16)
            q_scr[turn + 1, rows, :] = inner_scr[rows, :] * scale + q_scr[turn, rows, :] * (
                DAMPING * scale - 1.0
            )

    def turn_of(turn, is_first):
        receive(turn, is_first)
        stresses(turn)
        terms()
        scatter_shared(turn)
        scatter_inner()
        moment(2 * turn, turn, turn)
        if is_first:
            write_basis(turn)
            row = wait_sum(0, 1)
            total, squares = lane_of(row, 0), lane_of(row, 1)
            scale_scr[0:1, :] = 1.0 / (DAMPING + SHIFT_SCALE * squares / total)
            inner_rows(turn)
            gather_inner(turn + 1)
        else:
            inner_rows(turn)
            gather_inner(turn + 1)
            moment(2 * turn - 1, turn - 1, turn)
            write_basis(turn)

    turn_of(0, True)

    def body(turn, carry):
        turn_of(turn, False)
        return carry

    lax.fori_loop(1, ITERS - 1, body, 0)

    last = ITERS - 1
    receive(last, False)
    moment(2 * last - 1, last - 1, last)
    moment(2 * last, last, last)
    energy = stresses(last)
    moment_scr[pl.ds(2 * last + 1, 1), :] = jnp.sum(energy, axis=0, keepdims=True)
    send_sum(1, 0, row_of(moment_scr[...]))
    terms()
    scatter_shared(last)
    scatter_inner()
    send_sum(1, 1, wait_sum(1, 0))
    inner_rows(last)
    write_basis(last)
    receive(ITERS, False)
    write_basis(ITERS)
    row = wait_sum(1, 1)

    scale = scale_scr[0:1, :]
    m = [lane_of(row, k) for k in range(2 * ITERS)]
    m[2 * last + 1] = m[2 * last + 1] * scale + m[2 * last] * (DAMPING * scale - 1.0)
    low = [[None] * ITERS for _ in range(ITERS)]
    low_d = [[None] * ITERS for _ in range(ITERS)]
    inverse = [None] * ITERS
    right = [None] * ITERS
    for j in range(ITERS):
        pivot = m[2 * j]
        value = m[j + ITERS]
        for k in range(j):
            pivot = pivot - low[j][k] * low_d[j][k]
            value = value - low[j][k] * right[k]
        inverse[j] = 1.0 / pivot
        right[j] = value
        for i in range(j + 1, ITERS):
            entry = m[i + j]
            for k in range(j):
                entry = entry - low[i][k] * low_d[j][k]
            low_d[i][j] = entry
            low[i][j] = entry * inverse[j]
    coef = [None] * ITERS
    for i in reversed(range(ITERS)):
        value = right[i] * inverse[i]
        for k in range(i + 1, ITERS):
            value = value - low[k][i] * coef[k]
        coef[i] = value
    norm = -1.0
    for i in range(ITERS):
        norm = norm - coef[i] if i % 2 == 0 else norm + coef[i]
    by_norm = 1.0 / norm
    rest = [-value * by_norm for value in coef] + [by_norm]
    steps = [1.0 - rest[0]]
    for i in range(1, ITERS):
        steps.append(-rest[i] - steps[-1])
    rest = [jnp.broadcast_to(value, (8, 128)) for value in rest]
    steps = [jnp.broadcast_to(value * scale, (8, 128)) for value in steps]
    for r in range(NODE_ROWS):
        width = min(128, NODES - 128 * r)
        tiles = [basis_scr[i, :, 128 * r : 128 * r + 128] for i in range(ITERS + 1)]
        newton = tiles[0] * steps[0]
        for i in range(1, ITERS):
            newton = newton + tiles[i] * steps[i]
        left = tiles[0] * rest[0]
        for i in range(1, ITERS + 1):
            left = left + tiles[i] * rest[i]
        out_ref[0, :, 128 * r : 128 * r + width] = newton[0:3, 0:width]
        out_ref[1, :, 128 * r : 128 * r + width] = left[0:3, 0:width]

    for turn in range(ITERS + 1):
        pltpu.make_async_copy(recv_buf.at[turn], recv_buf.at[turn], halo_send.at[turn]).wait()
    for which in range(2):
        for stage in range(2):
            arrived = sum_in[stage].at[which]
            pltpu.make_async_copy(arrived, arrived, sum_send.at[2 * which + stage]).wait()


def shards(count, rhs_partial, connectivity, hessians, shared_nodes, owner):
    first, second = tables()
    sizes = [len(masks) for masks in stage_masks(count)]
    vmem = pltpu.VMEM
    out = pl.pallas_call(
        functools.partial(kernel, count),
        out_shape=vmem((2, 3, NODES), F32),
        in_specs=[pl.BlockSpec(memory_space=pltpu.HBM)] * 7,
        out_specs=pl.BlockSpec(memory_space=vmem),
        scratch_shapes=[
            vmem((3, NODES), F32),
            vmem((27, 128), jnp.int32),
            vmem((27, 45, 128), BF16),
            vmem((8, SHARE), jnp.int32),
            vmem((NODES,), jnp.int32),
            vmem(first.shape, BF16),
            vmem(second.shape, BF16),
            pltpu.SemaphoreType.DMA((7,)),
            vmem((48, 128), F32),
            vmem((16, 128), F32),
            vmem((8, 128), jnp.int32),
            vmem((16, 128), jnp.int32),
            vmem((32, 128), jnp.int32),
            vmem((32, 128), jnp.int32),
            vmem((32, 128), jnp.int32),
            vmem((27 * 128, 128), BF16),
            vmem((48 * 32, 128), F32),
            vmem((45, 32, 128), F32),
            vmem((ITERS + 1, 3 * ROWS, 128), F32),
            vmem((24, 128), F32),
            vmem((48, 128), F32),
            vmem((24, 128), F32),
            vmem((32, 384), F32),
            vmem((32, 384), F32),
            vmem((96, 384), F32),
            vmem((288, 384), BF16),
            vmem((3, 32, 384), F32),
            vmem((ROWS, 128), F32),
            vmem((16, 128), F32),
            vmem((8, 128), F32),
            vmem((ITERS + 1, 8, NODE_ROWS * 128), F32),
            vmem((ITERS + 1, BASE, 3, 1, 128), F32),
            vmem((ITERS + 1, PEERS, 3, 1, 128), F32),
            vmem((4, 1, 128), F32),
            vmem((2, sizes[0], 1, 128), F32),
            vmem((2, sizes[1], 1, 128), F32),
            pltpu.SemaphoreType.DMA((ITERS + 1,)),
            pltpu.SemaphoreType.DMA((ITERS + 1,)),
            pltpu.SemaphoreType.DMA((4,)),
            pltpu.SemaphoreType.DMA((4,)),
        ],
        compiler_params=pltpu.CompilerParams(collective_id=0, has_side_effects=True),
        name="newton_cg",
    )(
        rhs_partial,
        connectivity,
        jnp.transpose(hessians, (1, 0, 2)),
        shared_nodes,
        owner,
        jnp.asarray(first),
        jnp.asarray(second),
    )
    return out[0], out[1]


def solution(mesh):
    in_specs = (
        P(None, "parts"),
        P(None, "parts"),
        P(None, None, "parts"),
        P(None, "parts"),
        P("parts"),
    )
    out_specs = (P(None, "parts"), P(None, "parts"))
    return jax.shard_map(
        functools.partial(shards, mesh.shape["parts"]),
        mesh=mesh,
        in_specs=in_specs,
        out_specs=out_specs,
        check_vma=False,
    )
```

```python
import functools

import jax
import jax.numpy as jnp
import ml_dtypes
import numpy as np
from jax import lax
from jax.experimental import pallas as pl
from jax.experimental.pallas import tpu as pltpu
from jax.sharding import PartitionSpec as P

ITERS = 5
DAMPING = 2.0
MESH = pl.DeviceIdType.MESH
F32 = jnp.float32
BF16 = jnp.bfloat16

NODES = 1445
NODE_ROWS = 12
BASE = 4
ROWS = BASE + NODE_ROWS
PEERS = 8
SHARE = 34
PEER_ROW = [0, 0, 0, 2, 3, 1, 1, 1]
PEER_LANE = [0, 40, 80, 0, 0, 80, 40, 0]
SEND_ORDER = [0, 7, 1, 6, 2, 5, 3, 4]
SHIFT_SCALE = 0.045


def shape_table():
    points = np.array([-np.sqrt(0.6), 0.0, np.sqrt(0.6)])
    values = np.stack(
        [points * (points - 1.0) / 2.0, 1.0 - points * points, points * (points + 1.0) / 2.0],
        axis=1,
    )
    slopes = np.stack([points - 0.5, -2.0 * points, points + 0.5], axis=1)
    result = np.zeros((27, 3, 27))
    for direction in range(3):
        factors = [slopes if axis_index == direction else values for axis_index in range(3)]
        product = (
            factors[0][:, None, None, :, None, None]
            * factors[1][None, :, None, None, :, None]
            * factors[2][None, None, :, None, None, :]
        )
        result[:, direction, :] = product.reshape(27, 27)
    return result


def three_parts(table):
    rest = table.astype(np.float32)
    parts = []
    for _ in range(3):
        part = rest.astype(ml_dtypes.bfloat16)
        parts.append(part)
        rest = rest - part.astype(np.float32)
    return parts


def tables():
    table = shape_table()
    forward = np.zeros((3, 32, 32))
    forward[:, :27, :27] = table.transpose(1, 0, 2)
    high, mid, low = three_parts(forward.reshape(96, 32))
    first = np.concatenate([high, high, high, mid, mid, low], axis=1)
    weights = np.einsum("qda,qfa->dfq", table, table)
    row = np.zeros((16, 6, 32))
    for pair, (one, two) in enumerate(PAIRS):
        row[0, pair, :27] = weights[one, two] * (1.0 if one == two else 2.0)
    first = np.concatenate([first, row.reshape(16, 192).astype(ml_dtypes.bfloat16)], axis=0)
    high, mid, low = three_parts(forward.transpose(2, 0, 1).reshape(32, 96))
    zero = np.zeros_like(high)
    second = np.concatenate(
        [
            np.concatenate([high, high, high], axis=1),
            np.concatenate([mid, mid, zero], axis=1),
            np.concatenate([low, zero, zero], axis=1),
        ],
        axis=0,
    )
    return first, second


PAIRS = [(0, 0), (0, 1), (0, 2), (1, 1), (1, 2), (2, 2)]


def packed_index(row_index, col_index):
    first = min(row_index, col_index)
    second = max(row_index, col_index)
    return first * 9 - first * (first - 1) // 2 + (second - first)


def peer_offsets(count):
    half = count // 2
    return [offset - half for offset in range(half)] + [offset + 1 for offset in range(half)]


def links(mask):
    ring = [0, 1, 2, 3, 4, 3, 2, 3]
    return ring[(mask >> 1) & 7] + ring[(mask >> 4) & 7] + [0, 1, 2, 1][(mask >> 7) & 3]


def stage_masks(count):
    bits = count.bit_length() - 1
    low = 1 << min(4, bits - 1)
    masks = [list(range(1, low)), [low * k for k in range(1, count // low)]]
    return [sorted(stage, key=lambda mask: -links(mask)) for stage in masks]


def parts_of(value):
    high = value.astype(BF16).astype(F32)
    rest = value - high
    mid = rest.astype(BF16).astype(F32)
    return high, mid, (rest - mid).astype(BF16).astype(F32)


def lane_of(row, lane):
    return jnp.broadcast_to(row[:, lane : lane + 1], (1, 128))


def spread(ref, row):
    return jnp.broadcast_to(ref[pl.ds(row, 1), :], (8, 128))


def pick(ref, base, count, first, rows, lanes, start):
    result = start
    for row in range(count):
        found = jnp.take_along_axis(spread(ref, base + row), lanes, axis=1)
        result = jnp.where(rows == first + row, found, result)
    return result


def kernel(
    count,
    rhs_hbm,
    conn_hbm,
    hess_hbm,
    shared_hbm,
    owner_hbm,
    first_hbm,
    second_hbm,
    out_ref,
    rhs_ref,
    conn_ref,
    hess_ref,
    shared_ref,
    owner_ref,
    first_ref,
    second_ref,
    load_sem,
    nodes_scr,
    owner_scr,
    shared_scr,
    map_scr,
    conn_scr,
    row_scr,
    lane_scr,
    hot_scr,
    wide_scr,
    h_scr,
    q_scr,
    own_scr,
    inner_scr,
    in_scr,
    part_scr,
    u_scr,
    g_scr,
    s_scr,
    t_scr,
    weight_scr,
    moment_scr,
    scale_scr,
    basis_scr,
    send_buf,
    recv_buf,
    sum_out,
    sum_in0,
    sum_in1,
    halo_send,
    halo_recv,
    sum_send,
    sum_recv,
):
    me = lax.axis_index("parts")
    peers = [(me + offset) & (count - 1) for offset in peer_offsets(PEERS)]
    stages = [[me ^ mask for mask in masks] for masks in stage_masks(count)]
    sum_in = [sum_in0, sum_in1]

    barrier = pltpu.get_barrier_semaphore()
    everyone = peers + stages[0] + stages[1]
    for other in everyone:
        pl.semaphore_signal(barrier, inc=1, device_id=(other,), device_id_type=MESH)

    loads = [
        pltpu.make_async_copy(source, target, load_sem.at[i])
        for i, (source, target) in enumerate(
            [
                (rhs_hbm, rhs_ref),
                (shared_hbm, shared_ref),
                (owner_hbm, owner_ref),
                (hess_hbm, hess_ref),
                (first_hbm, first_ref),
                (conn_hbm, conn_ref),
                (second_hbm, second_ref),
            ]
        )
    ]
    for load in loads:
        load.start()

    sublane = lax.broadcasted_iota(jnp.int32, (8, 128), 0)
    lane = lax.broadcasted_iota(jnp.int32, (8, 128), 1)
    sublane16 = lax.broadcasted_iota(jnp.int32, (16, 128), 0)

    def send_halo(turn):
        for j in SEND_ORDER:
            pltpu.make_async_remote_copy(
                src_ref=send_buf.at[turn, PEER_ROW[j]],
                dst_ref=recv_buf.at[turn, PEERS - 1 - j],
                send_sem=halo_send.at[turn],
                recv_sem=halo_recv.at[turn],
                device_id=(peers[j],),
                device_id_type=MESH,
            ).start()

    def wait_halo(turn):
        pltpu.make_async_copy(recv_buf.at[turn], recv_buf.at[turn], halo_recv.at[turn]).wait()

    def send_sum(which, stage, row):
        slot = 2 * which + stage
        sum_out[slot] = row
        for k, other in enumerate(stages[stage]):
            pltpu.make_async_remote_copy(
                src_ref=sum_out.at[slot],
                dst_ref=sum_in[stage].at[which, k],
                send_sem=sum_send.at[slot],
                recv_sem=sum_recv.at[slot],
                device_id=(other,),
                device_id_type=MESH,
            ).start()

    def wait_sum(which, stage):
        slot = 2 * which + stage
        arrived = sum_in[stage].at[which]
        pltpu.make_async_copy(arrived, arrived, sum_recv.at[slot]).wait()
        terms = [sum_out[slot]] + [sum_in[stage][which, k] for k in range(len(stages[stage]))]
        while len(terms) > 1:
            terms = [sum(terms[i : i + 2]) for i in range(0, len(terms), 2)]
        return terms[0]

    nodes_scr[...] = jnp.zeros_like(nodes_scr)
    owner_scr[...] = jnp.zeros_like(owner_scr)
    for load in loads[0:3]:
        load.wait()
    for r in range(NODE_ROWS):
        width = min(128, NODES - 128 * r)
        for c in range(3):
            nodes_scr[pl.ds(16 * c + BASE + r, 1), 0:width] = rhs_ref[c : c + 1, 128 * r : 128 * r + width]
        owner_scr[pl.ds(BASE + r, 1), 0:width] = owner_ref[128 * r : 128 * r + width].reshape(1, width).astype(F32)
    shared_scr[...] = jnp.full((8, 128), NODES, jnp.int32)
    for j in range(PEERS):
        start = PEER_LANE[j]
        shared_scr[PEER_ROW[j] : PEER_ROW[j] + 1, start : start + SHARE] = shared_ref[j : j + 1, :]
    names = shared_scr[...]
    used = names < NODES
    name_rows, name_lanes = (names >> 7) + BASE, names & 127
    zero = jnp.zeros((8, 128), F32)
    for c in range(3):
        found = pick(nodes_scr, 16 * c + BASE, NODE_ROWS, BASE, name_rows, name_lanes, zero)
        own_scr[pl.ds(8 * c, 8), :] = jnp.where(used, found, 0.0)
    owned = pick(owner_scr, BASE, NODE_ROWS, BASE, name_rows, name_lanes, zero)
    shared_weight = jnp.where(used, owned, 0.0)

    def fill_message(turn):
        for c in range(3):
            for row in range(BASE):
                send_buf[turn, row, c] = own_scr[pl.ds(8 * c + row, 1), :]

    fill_message(0)
    pl.semaphore_wait(barrier, len(everyone))
    send_halo(0)

    for load in loads[3:]:
        load.wait()
    for q in range(27):
        wide_scr[48 * q : 48 * q + 45, :] = hess_ref[q].astype(F32)
    wide_scr[48 * 27 :, :] = jnp.zeros((48 * 5, 128), F32)
    for k in range(45):
        for t in range(4):
            h_scr[k, 8 * t : 8 * t + 8, :] = wide_scr[pl.ds(48 * 8 * t + k, 8, stride=48), :]
    sums = []
    for one, two in PAIRS:
        total = h_scr[packed_index(one, two)]
        for i in range(1, 3):
            total = total + h_scr[packed_index(3 * i + one, 3 * i + two)]
        sums.append(total)
    stacked = jnp.concatenate(sums, axis=0).astype(BF16)
    traces = jnp.dot(first_ref[96:112, :], stacked, preferred_element_type=F32)[0:1, :]

    def row_of(values):
        totals = jnp.sum(values, axis=1, keepdims=True)
        rows = lax.broadcasted_iota(jnp.int32, values.shape, 0)
        lanes = lax.broadcasted_iota(jnp.int32, values.shape, 1)
        return jnp.sum(jnp.where(rows == lanes, totals, 0.0), axis=0, keepdims=True)

    both = jnp.where(sublane == 0, traces, jnp.where(sublane == 1, traces * traces, 0.0))
    send_sum(0, 0, row_of(both))

    found = jnp.zeros((32, 128), F32)
    for j in range(BASE):
        rows_j = jnp.broadcast_to(jnp.where(used, name_rows, 99)[j : j + 1, :], (16, 128))
        lanes_j = jnp.broadcast_to(name_lanes[j : j + 1, :], (128, 128))
        hit = rows_j == sublane16
        slot = lax.broadcasted_iota(jnp.int32, (16, 128), 1).astype(F32)
        left = jnp.concatenate(
            [jnp.where(hit, float(j + 1), 0.0), jnp.where(hit, slot, 0.0)], axis=0
        )
        right = jnp.where(
            lanes_j == lax.broadcasted_iota(jnp.int32, (128, 128), 0), 1.0, 0.0
        )
        found = found + lax.dot_general(
            left.astype(BF16),
            right.astype(BF16),
            (((1,), (1,)), ((), ())),
            preferred_element_type=F32,
        )
    map_scr[...] = (128.0 * found[0:16] + found[16:32]).astype(jnp.int32)
    others = jnp.where(map_scr[...] > 0, 0.0, owner_scr[...])
    weight_scr[0:8, :] = others[0:8] + shared_weight
    weight_scr[8:16, :] = others[8:16]

    conn_scr[...] = jnp.zeros_like(conn_scr)
    conn_scr[0:27, :] = conn_ref[...]
    for t in range(4):
        names_t = conn_scr[pl.ds(8 * t, 8), :]
        rows_t, lanes_t = (names_t >> 7) + BASE, names_t & 127
        where_t = pick(map_scr, BASE, NODE_ROWS, BASE, rows_t, lanes_t, jnp.zeros((8, 128), jnp.int32))
        is_shared = where_t > 0
        row_t = jnp.where(is_shared, (where_t >> 7) - 1, rows_t)
        if t == 3:
            row_t = jnp.where(sublane < 3, row_t, 99)
        row_scr[pl.ds(8 * t, 8), :] = row_t
        lane_scr[pl.ds(8 * t, 8), :] = jnp.where(is_shared, where_t & 127, lanes_t)

    columns = jnp.transpose(lane_scr[...].astype(F32))
    lanes_all = lax.broadcasted_iota(jnp.int32, (128, 128), 1).astype(F32)
    for a in range(27):
        column = jnp.broadcast_to(columns[:, a : a + 1], (128, 128))
        hot_scr[pl.ds(128 * a, 128), :] = jnp.where(column == lanes_all, 1.0, 0.0).astype(BF16)

    for c in range(3):
        q_scr[0, pl.ds(16 * c, 16), :] = jnp.where(
            map_scr[...] > 0, 0.0, nodes_scr[pl.ds(16 * c, 16), :]
        )
    moment_scr[...] = jnp.zeros_like(moment_scr)

    def gather_inner(turn):
        for t in range(4):
            rows_t = row_scr[pl.ds(8 * t, 8), :]
            lanes_t = lane_scr[pl.ds(8 * t, 8), :]
            for c in range(3):
                part_scr[pl.ds(8 * t, 8), 128 * c : 128 * c + 128] = pick(
                    q_scr.at[turn], 16 * c + BASE, NODE_ROWS, BASE, rows_t, lanes_t, zero
                )

    gather_inner(0)
    send_sum(0, 1, wait_sum(0, 0))

    def moment(index, one, two):
        total = zero
        for c in range(3):
            for t in range(2):
                rows = pl.ds(16 * c + 8 * t, 8)
                total = total + weight_scr[pl.ds(8 * t, 8), :] * q_scr[one, rows, :] * q_scr[two, rows, :]
        moment_scr[pl.ds(index, 1), :] = jnp.sum(total, axis=0, keepdims=True)

    def write_basis(turn):
        for t in range(2):
            where_t = map_scr[pl.ds(8 * t, 8), :]
            rows_t, lanes_t = (where_t >> 7) - 1, where_t & 127
            for c in range(3):
                inner = q_scr[turn, pl.ds(16 * c + 8 * t, 8), :]
                value = pick(q_scr.at[turn], 16 * c, BASE, 0, rows_t, lanes_t, inner)
                for row in range(BASE if t == 0 else 0, 8):
                    start = 128 * (8 * t + row - BASE)
                    basis_scr[turn, pl.ds(c, 1), start : start + 128] = value[row : row + 1, :]

    def receive(turn, is_first):
        wait_halo(turn)
        lanes = lax.broadcasted_iota(jnp.int32, (1, 128), 1)
        for c in range(3):
            arrived = [recv_buf[turn, j, c] for j in range(PEERS)]
            for row in range(BASE):
                own = [j for j in range(PEERS) if PEER_ROW[j] == row]
                own.sort(key=lambda j: PEER_LANE[j])
                value = arrived[own[0]]
                for j in own[1:]:
                    value = jnp.where(lanes >= PEER_LANE[j], arrived[j], value)
                in_scr[pl.ds(8 * c + row, 1), :] = value
        for c in range(3):
            value = own_scr[pl.ds(8 * c, BASE), :] + in_scr[pl.ds(8 * c, BASE), :]
            if not is_first:
                before = q_scr[turn - 1, pl.ds(16 * c, BASE), :]
                scale = jnp.broadcast_to(scale_scr[0:1, :], (BASE, 128))
                value = value * scale + before * (DAMPING * scale - 1.0)
            q_scr[turn, pl.ds(16 * c, BASE), :] = value

    def stresses(turn):
        for t in range(4):
            rows_t = row_scr[pl.ds(8 * t, 8), :]
            lanes_t = lane_scr[pl.ds(8 * t, 8), :]
            for c in range(3):
                u_scr[pl.ds(8 * t, 8), 128 * c : 128 * c + 128] = pick(
                    q_scr.at[turn],
                    16 * c,
                    BASE,
                    0,
                    rows_t,
                    lanes_t,
                    part_scr[pl.ds(8 * t, 8), 128 * c : 128 * c + 128],
                )
        high, mid, low = parts_of(u_scr[...])
        right = jnp.concatenate([high, mid, low, high, mid, high], axis=0).astype(BF16)
        g_scr[...] = jnp.dot(first_ref[0:96, :], right, preferred_element_type=F32)
        energy = zero
        for t in range(2):
            grads = [
                g_scr[32 * (n % 3) + 16 * t : 32 * (n % 3) + 16 * t + 16, 128 * (n // 3) : 128 * (n // 3) + 128]
                for n in range(9)
            ]
            for m in range(9):
                total = h_scr[packed_index(m, 0), pl.ds(16 * t, 16), :] * grads[0]
                for n in range(1, 9):
                    total = total + h_scr[packed_index(m, n), pl.ds(16 * t, 16), :] * grads[n]
                product = total * grads[m]
                energy = energy + product[0:8] + product[8:16]
                for p, part in enumerate(parts_of(total)):
                    row = 96 * p + 32 * (m % 3) + 16 * t
                    s_scr[row : row + 16, 128 * (m // 3) : 128 * (m // 3) + 128] = part.astype(BF16)
        return energy

    def terms():
        blocks = jnp.dot(second_ref[...], s_scr[...], preferred_element_type=F32)
        summed = blocks[0:32] + blocks[32:64] + blocks[64:96]
        for p, part in enumerate(parts_of(summed)):
            t_scr[p] = part

    def term(p, a, c, height):
        row = t_scr[p, pl.ds(a, 1), 128 * c : 128 * c + 128]
        return jnp.broadcast_to(row, (height, 128))

    def by_lane(left):
        summed = None
        for a in range(0, 27, 4):
            part = jnp.dot(
                jnp.concatenate(left[a : a + 4], axis=1),
                hot_scr[128 * a : 128 * min(a + 4, 27), :],
                preferred_element_type=F32,
            )
            summed = part if summed is None else summed + part
        return summed

    def scatter_shared(turn):
        order = [(c, p) for c in range(3) for p in range(3)]
        upper = sublane < BASE
        numbers = sublane & (BASE - 1)
        left = []
        for a in range(27):
            mask = spread(row_scr, a) == numbers
            tiles = []
            for i in range(0, 9, 2):
                value = term(order[i][1], a, order[i][0], 8)
                if i < 8:
                    other = term(order[i + 1][1], a, order[i + 1][0], 8)
                    tiles.append(jnp.where(mask, jnp.where(upper, value, other), 0.0))
                else:
                    tiles.append(jnp.where(mask & upper, value, 0.0))
            tiles.append(zero)
            left.append(jnp.concatenate(tiles, axis=0).astype(BF16))
        summed = by_lane(left)
        for c in range(3):
            own_scr[pl.ds(8 * c, BASE), :] = (
                summed[12 * c : 12 * c + 4]
                + summed[12 * c + 4 : 12 * c + 8]
                + summed[12 * c + 8 : 12 * c + 12]
            )
        fill_message(turn + 1)
        send_halo(turn + 1)

    def scatter_inner():
        left = []
        for a in range(27):
            mask = jnp.broadcast_to(row_scr[pl.ds(a, 1), :], (16, 128)) == sublane16
            tiles = [jnp.where(mask, term(p, a, c, 16), 0.0) for c in range(3) for p in range(3)]
            left.append(jnp.concatenate(tiles, axis=0).astype(BF16))
        summed = by_lane(left)
        for c in range(3):
            inner_scr[pl.ds(16 * c, 16), :] = (
                summed[48 * c : 48 * c + 16]
                + summed[48 * c + 16 : 48 * c + 32]
                + summed[48 * c + 32 : 48 * c + 48]
            )

    def inner_rows(turn):
        scale = jnp.broadcast_to(scale_scr[0:1, :], (16, 128))
        for c in range(3):
            rows = pl.ds(16 * c, 16)
            q_scr[turn + 1, rows, :] = inner_scr[rows, :] * scale + q_scr[turn, rows, :] * (
                DAMPING * scale - 1.0
            )

    def turn_of(turn, is_first):
        receive(turn, is_first)
        stresses(turn)
        terms()
        scatter_shared(turn)
        scatter_inner()
        moment(2 * turn, turn, turn)
        if is_first:
            write_basis(turn)
            row = wait_sum(0, 1)
            total, squares = lane_of(row, 0), lane_of(row, 1)
            scale_scr[0:1, :] = 1.0 / (DAMPING + SHIFT_SCALE * squares / total)
            inner_rows(turn)
            gather_inner(turn + 1)
        else:
            inner_rows(turn)
            gather_inner(turn + 1)
            moment(2 * turn - 1, turn - 1, turn)
            write_basis(turn)

    turn_of(0, True)

    def body(turn, carry):
        turn_of(turn, False)
        return carry

    lax.fori_loop(1, ITERS - 1, body, 0)

    last = ITERS - 1
    receive(last, False)
    moment(2 * last - 1, last - 1, last)
    moment(2 * last, last, last)
    known = row_of(moment_scr[...])
    energy = jnp.sum(stresses(last), axis=0, keepdims=True)
    total = jnp.sum(energy, axis=1, keepdims=True)
    send_sum(1, 0, jnp.where(lane[0:1, :] == 2 * last + 1, total, known))
    terms()
    scatter_shared(last)
    scatter_inner()
    send_sum(1, 1, wait_sum(1, 0))
    inner_rows(last)
    write_basis(last)
    receive(ITERS, False)
    write_basis(ITERS)
    row = wait_sum(1, 1)

    scale = scale_scr[0:1, :]
    m = [lane_of(row, k) for k in range(2 * ITERS)]
    m[2 * last + 1] = m[2 * last + 1] * scale + m[2 * last] * (DAMPING * scale - 1.0)
    low = [[None] * ITERS for _ in range(ITERS)]
    low_d = [[None] * ITERS for _ in range(ITERS)]
    inverse = [None] * ITERS
    right = [None] * ITERS
    for j in range(ITERS):
        pivot = m[2 * j]
        value = m[j + ITERS]
        for k in range(j):
            pivot = pivot - low[j][k] * low_d[j][k]
            value = value - low[j][k] * right[k]
        inverse[j] = 1.0 / pivot
        right[j] = value
        for i in range(j + 1, ITERS):
            entry = m[i + j]
            for k in range(j):
                entry = entry - low[i][k] * low_d[j][k]
            low_d[i][j] = entry
            low[i][j] = entry * inverse[j]
    coef = [None] * ITERS
    for i in reversed(range(ITERS)):
        value = right[i] * inverse[i]
        for k in range(i + 1, ITERS):
            value = value - low[k][i] * coef[k]
        coef[i] = value
    norm = -1.0
    for i in range(ITERS):
        norm = norm - coef[i] if i % 2 == 0 else norm + coef[i]
    by_norm = 1.0 / norm
    rest = [-value * by_norm for value in coef] + [by_norm]
    steps = [1.0 - rest[0]]
    for i in range(1, ITERS):
        steps.append(-rest[i] - steps[-1])
    rest = [jnp.broadcast_to(value, (8, 128)) for value in rest]
    steps = [jnp.broadcast_to(value * scale, (8, 128)) for value in steps]
    for r in range(NODE_ROWS):
        width = min(128, NODES - 128 * r)
        tiles = [basis_scr[i, :, 128 * r : 128 * r + 128] for i in range(ITERS + 1)]
        newton = tiles[0] * steps[0]
        for i in range(1, ITERS):
            newton = newton + tiles[i] * steps[i]
        left = tiles[0] * rest[0]
        for i in range(1, ITERS + 1):
            left = left + tiles[i] * rest[i]
        out_ref[0, :, 128 * r : 128 * r + width] = newton[0:3, 0:width]
        out_ref[1, :, 128 * r : 128 * r + width] = left[0:3, 0:width]

    for turn in range(ITERS + 1):
        pltpu.make_async_copy(recv_buf.at[turn], recv_buf.at[turn], halo_send.at[turn]).wait()
    for which in range(2):
        for stage in range(2):
            arrived = sum_in[stage].at[which]
            pltpu.make_async_copy(arrived, arrived, sum_send.at[2 * which + stage]).wait()


def shards(count, rhs_partial, connectivity, hessians, shared_nodes, owner):
    first, second = tables()
    sizes = [len(masks) for masks in stage_masks(count)]
    vmem = pltpu.VMEM
    out = pl.pallas_call(
        functools.partial(kernel, count),
        out_shape=vmem((2, 3, NODES), F32),
        in_specs=[pl.BlockSpec(memory_space=pltpu.HBM)] * 7,
        out_specs=pl.BlockSpec(memory_space=vmem),
        scratch_shapes=[
            vmem((3, NODES), F32),
            vmem((27, 128), jnp.int32),
            vmem((27, 45, 128), BF16),
            vmem((8, SHARE), jnp.int32),
            vmem((NODES,), jnp.int32),
            vmem(first.shape, BF16),
            vmem(second.shape, BF16),
            pltpu.SemaphoreType.DMA((7,)),
            vmem((48, 128), F32),
            vmem((16, 128), F32),
            vmem((8, 128), jnp.int32),
            vmem((16, 128), jnp.int32),
            vmem((32, 128), jnp.int32),
            vmem((32, 128), jnp.int32),
            vmem((32, 128), jnp.int32),
            vmem((27 * 128, 128), BF16),
            vmem((48 * 32, 128), F32),
            vmem((45, 32, 128), F32),
            vmem((ITERS + 1, 3 * ROWS, 128), F32),
            vmem((24, 128), F32),
            vmem((48, 128), F32),
            vmem((24, 128), F32),
            vmem((32, 384), F32),
            vmem((32, 384), F32),
            vmem((96, 384), F32),
            vmem((288, 384), BF16),
            vmem((3, 32, 384), F32),
            vmem((ROWS, 128), F32),
            vmem((16, 128), F32),
            vmem((8, 128), F32),
            vmem((ITERS + 1, 8, NODE_ROWS * 128), F32),
            vmem((ITERS + 1, BASE, 3, 1, 128), F32),
            vmem((ITERS + 1, PEERS, 3, 1, 128), F32),
            vmem((4, 1, 128), F32),
            vmem((2, sizes[0], 1, 128), F32),
            vmem((2, sizes[1], 1, 128), F32),
            pltpu.SemaphoreType.DMA((ITERS + 1,)),
            pltpu.SemaphoreType.DMA((ITERS + 1,)),
            pltpu.SemaphoreType.DMA((4,)),
            pltpu.SemaphoreType.DMA((4,)),
        ],
        compiler_params=pltpu.CompilerParams(collective_id=0, has_side_effects=True),
        name="newton_cg",
    )(
        rhs_partial,
        connectivity,
        jnp.transpose(hessians, (1, 0, 2)),
        shared_nodes,
        owner,
        jnp.asarray(first),
        jnp.asarray(second),
    )
    return out[0], out[1]


def solution(mesh):
    in_specs = (
        P(None, "parts"),
        P(None, "parts"),
        P(None, None, "parts"),
        P(None, "parts"),
        P("parts"),
    )
    out_specs = (P(None, "parts"), P(None, "parts"))
    return jax.shard_map(
        functools.partial(shards, mesh.shape["parts"]),
        mesh=mesh,
        in_specs=in_specs,
        out_specs=out_specs,
        check_vma=False,
    )
```

```python
import functools

import jax
import jax.numpy as jnp
import ml_dtypes
import numpy as np
from jax import lax
from jax.experimental import pallas as pl
from jax.experimental.pallas import tpu as pltpu
from jax.sharding import PartitionSpec as P

ITERS = 5
DAMPING = 2.0
MESH = pl.DeviceIdType.MESH
F32 = jnp.float32
BF16 = jnp.bfloat16

NODES = 1445
NODE_ROWS = 12
BASE = 4
ROWS = BASE + NODE_ROWS
PEERS = 8
SHARE = 34
PEER_ROW = [0, 0, 0, 2, 3, 1, 1, 1]
PEER_LANE = [0, 40, 80, 0, 0, 80, 40, 0]
SEND_ORDER = [0, 7, 1, 6, 2, 5, 3, 4]
SHIFT_SCALE = 0.045


def shape_table():
    points = np.array([-np.sqrt(0.6), 0.0, np.sqrt(0.6)])
    values = np.stack(
        [points * (points - 1.0) / 2.0, 1.0 - points * points, points * (points + 1.0) / 2.0],
        axis=1,
    )
    slopes = np.stack([points - 0.5, -2.0 * points, points + 0.5], axis=1)
    result = np.zeros((27, 3, 27))
    for direction in range(3):
        factors = [slopes if axis_index == direction else values for axis_index in range(3)]
        product = (
            factors[0][:, None, None, :, None, None]
            * factors[1][None, :, None, None, :, None]
            * factors[2][None, None, :, None, None, :]
        )
        result[:, direction, :] = product.reshape(27, 27)
    return result


def three_parts(table):
    rest = table.astype(np.float32)
    parts = []
    for _ in range(3):
        part = rest.astype(ml_dtypes.bfloat16)
        parts.append(part)
        rest = rest - part.astype(np.float32)
    return parts


def tables():
    table = shape_table()
    forward = np.zeros((3, 32, 32))
    forward[:, :27, :27] = table.transpose(1, 0, 2)
    high, mid, low = three_parts(forward.reshape(96, 32))
    first = np.concatenate([high, high, high, mid, mid, low], axis=1)
    weights = np.einsum("qda,qfa->dfq", table, table)
    row = np.zeros((16, 6, 32))
    for pair, (one, two) in enumerate(PAIRS):
        row[0, pair, :27] = weights[one, two] * (1.0 if one == two else 2.0)
    first = np.concatenate([first, row.reshape(16, 192).astype(ml_dtypes.bfloat16)], axis=0)
    high, mid, low = three_parts(forward.transpose(2, 0, 1).reshape(32, 96))
    zero = np.zeros_like(high)
    second = np.concatenate(
        [
            np.concatenate([high, high, high], axis=1),
            np.concatenate([mid, mid, zero], axis=1),
            np.concatenate([low, zero, zero], axis=1),
        ],
        axis=0,
    )
    return first, second


PAIRS = [(0, 0), (0, 1), (0, 2), (1, 1), (1, 2), (2, 2)]


def packed_index(row_index, col_index):
    first = min(row_index, col_index)
    second = max(row_index, col_index)
    return first * 9 - first * (first - 1) // 2 + (second - first)


def peer_offsets(count):
    half = count // 2
    return [offset - half for offset in range(half)] + [offset + 1 for offset in range(half)]


def links(mask):
    ring = [0, 1, 2, 3, 4, 3, 2, 3]
    return ring[(mask >> 1) & 7] + ring[(mask >> 4) & 7] + [0, 1, 2, 1][(mask >> 7) & 3]


def stage_masks(count):
    bits = count.bit_length() - 1
    low = 1 << min(4, bits - 1)
    masks = [list(range(1, low)), [low * k for k in range(1, count // low)]]
    return [sorted(stage, key=lambda mask: -links(mask)) for stage in masks]


def parts_of(value):
    high = value.astype(BF16).astype(F32)
    rest = value - high
    mid = rest.astype(BF16).astype(F32)
    return high, mid, (rest - mid).astype(BF16).astype(F32)


def lane_of(row, lane):
    return jnp.broadcast_to(row[:, lane : lane + 1], (1, 128))


def spread(ref, row):
    return jnp.broadcast_to(ref[pl.ds(row, 1), :], (8, 128))


def pick(ref, base, count, first, rows, lanes, start):
    result = start
    for row in range(count):
        found = jnp.take_along_axis(spread(ref, base + row), lanes, axis=1)
        result = jnp.where(rows == first + row, found, result)
    return result


def kernel(
    count,
    rhs_hbm,
    conn_hbm,
    hess_hbm,
    shared_hbm,
    owner_hbm,
    first_hbm,
    second_hbm,
    out_ref,
    rhs_ref,
    conn_ref,
    hess_ref,
    shared_ref,
    owner_ref,
    first_ref,
    second_ref,
    load_sem,
    nodes_scr,
    owner_scr,
    shared_scr,
    map_scr,
    conn_scr,
    row_scr,
    lane_scr,
    hot_scr,
    wide_scr,
    h_scr,
    q_scr,
    own_scr,
    inner_scr,
    in_scr,
    part_scr,
    u_scr,
    g_scr,
    s_scr,
    t_scr,
    weight_scr,
    moment_scr,
    scale_scr,
    basis_scr,
    send_buf,
    recv_buf,
    sum_out,
    sum_in0,
    sum_in1,
    halo_send,
    halo_recv,
    sum_send,
    sum_recv,
):
    me = lax.axis_index("parts")
    peers = [(me + offset) & (count - 1) for offset in peer_offsets(PEERS)]
    stages = [[me ^ mask for mask in masks] for masks in stage_masks(count)]
    sum_in = [sum_in0, sum_in1]

    barrier = pltpu.get_barrier_semaphore()
    everyone = peers + stages[0] + stages[1]
    for other in everyone:
        pl.semaphore_signal(barrier, inc=1, device_id=(other,), device_id_type=MESH)

    loads = [
        pltpu.make_async_copy(source, target, load_sem.at[i])
        for i, (source, target) in enumerate(
            [
                (rhs_hbm, rhs_ref),
                (shared_hbm, shared_ref),
                (owner_hbm, owner_ref),
                (hess_hbm, hess_ref),
                (first_hbm, first_ref),
                (conn_hbm, conn_ref),
                (second_hbm, second_ref),
            ]
        )
    ]
    for load in loads:
        load.start()

    sublane = lax.broadcasted_iota(jnp.int32, (8, 128), 0)
    lane = lax.broadcasted_iota(jnp.int32, (8, 128), 1)
    sublane16 = lax.broadcasted_iota(jnp.int32, (16, 128), 0)

    def send_halo(turn):
        for j in SEND_ORDER:
            pltpu.make_async_remote_copy(
                src_ref=send_buf.at[turn, PEER_ROW[j]],
                dst_ref=recv_buf.at[turn, PEERS - 1 - j],
                send_sem=halo_send.at[turn],
                recv_sem=halo_recv.at[turn],
                device_id=(peers[j],),
                device_id_type=MESH,
            ).start()

    def wait_halo(turn):
        pltpu.make_async_copy(recv_buf.at[turn], recv_buf.at[turn], halo_recv.at[turn]).wait()

    def send_sum(which, stage, row):
        slot = 2 * which + stage
        sum_out[slot] = row
        for k, other in enumerate(stages[stage]):
            pltpu.make_async_remote_copy(
                src_ref=sum_out.at[slot],
                dst_ref=sum_in[stage].at[which, k],
                send_sem=sum_send.at[slot],
                recv_sem=sum_recv.at[slot],
                device_id=(other,),
                device_id_type=MESH,
            ).start()

    def wait_sum(which, stage):
        slot = 2 * which + stage
        arrived = sum_in[stage].at[which]
        pltpu.make_async_copy(arrived, arrived, sum_recv.at[slot]).wait()
        terms = [sum_out[slot]] + [sum_in[stage][which, k] for k in range(len(stages[stage]))]
        while len(terms) > 1:
            terms = [sum(terms[i : i + 2]) for i in range(0, len(terms), 2)]
        return terms[0]

    nodes_scr[...] = jnp.zeros_like(nodes_scr)
    owner_scr[...] = jnp.zeros_like(owner_scr)
    for load in loads[0:3]:
        load.wait()
    for r in range(NODE_ROWS):
        width = min(128, NODES - 128 * r)
        for c in range(3):
            nodes_scr[pl.ds(16 * c + BASE + r, 1), 0:width] = rhs_ref[c : c + 1, 128 * r : 128 * r + width]
        owner_scr[pl.ds(BASE + r, 1), 0:width] = owner_ref[128 * r : 128 * r + width].reshape(1, width).astype(F32)
    shared_scr[...] = jnp.full((8, 128), NODES, jnp.int32)
    for j in range(PEERS):
        start = PEER_LANE[j]
        shared_scr[PEER_ROW[j] : PEER_ROW[j] + 1, start : start + SHARE] = shared_ref[j : j + 1, :]
    names = shared_scr[...]
    used = names < NODES
    name_rows, name_lanes = (names >> 7) + BASE, names & 127
    zero = jnp.zeros((8, 128), F32)
    for c in range(3):
        found = pick(nodes_scr, 16 * c + BASE, NODE_ROWS, BASE, name_rows, name_lanes, zero)
        own_scr[pl.ds(8 * c, 8), :] = jnp.where(used, found, 0.0)
    owned = pick(owner_scr, BASE, NODE_ROWS, BASE, name_rows, name_lanes, zero)
    shared_weight = jnp.where(used, owned, 0.0)

    def fill_message(turn):
        for c in range(3):
            for row in range(BASE):
                send_buf[turn, row, c] = own_scr[pl.ds(8 * c + row, 1), :]

    fill_message(0)
    pl.semaphore_wait(barrier, len(everyone))
    send_halo(0)

    for load in loads[3:]:
        load.wait()
    for q in range(27):
        wide_scr[48 * q : 48 * q + 45, :] = hess_ref[q].astype(F32)
    wide_scr[48 * 27 : 48 * 32, :] = jnp.zeros((48 * 5, 128), F32)
    for k in range(45):
        for t in range(4):
            h_scr[k, 8 * t : 8 * t + 8, :] = wide_scr[pl.ds(48 * 8 * t + k, 8, stride=48), :]
    sums = []
    for one, two in PAIRS:
        total = h_scr[packed_index(one, two)]
        for i in range(1, 3):
            total = total + h_scr[packed_index(3 * i + one, 3 * i + two)]
        sums.append(total)
    stacked = jnp.concatenate(sums, axis=0).astype(BF16)
    traces = jnp.dot(first_ref[96:112, :], stacked, preferred_element_type=F32)[0:1, :]

    def row_of(values):
        totals = jnp.sum(values, axis=1, keepdims=True)
        rows = lax.broadcasted_iota(jnp.int32, values.shape, 0)
        lanes = lax.broadcasted_iota(jnp.int32, values.shape, 1)
        return jnp.sum(jnp.where(rows == lanes, totals, 0.0), axis=0, keepdims=True)

    both = jnp.where(sublane == 0, traces, jnp.where(sublane == 1, traces * traces, 0.0))
    send_sum(0, 0, row_of(both))

    found = jnp.zeros((32, 128), F32)
    for j in range(BASE):
        rows_j = jnp.broadcast_to(jnp.where(used, name_rows, 99)[j : j + 1, :], (16, 128))
        lanes_j = jnp.broadcast_to(name_lanes[j : j + 1, :], (128, 128))
        hit = rows_j == sublane16
        slot = lax.broadcasted_iota(jnp.int32, (16, 128), 1).astype(F32)
        left = jnp.concatenate(
            [jnp.where(hit, float(j + 1), 0.0), jnp.where(hit, slot, 0.0)], axis=0
        )
        right = jnp.where(
            lanes_j == lax.broadcasted_iota(jnp.int32, (128, 128), 0), 1.0, 0.0
        )
        found = found + lax.dot_general(
            left.astype(BF16),
            right.astype(BF16),
            (((1,), (1,)), ((), ())),
            preferred_element_type=F32,
        )
    map_scr[...] = (128.0 * found[0:16] + found[16:32]).astype(jnp.int32)
    others = jnp.where(map_scr[...] > 0, 0.0, owner_scr[...])
    weight_scr[0:8, :] = others[0:8] + shared_weight
    weight_scr[8:16, :] = others[8:16]

    conn_scr[...] = jnp.zeros_like(conn_scr)
    conn_scr[0:27, :] = conn_ref[...]
    for t in range(4):
        names_t = conn_scr[pl.ds(8 * t, 8), :]
        rows_t, lanes_t = (names_t >> 7) + BASE, names_t & 127
        where_t = pick(map_scr, BASE, NODE_ROWS, BASE, rows_t, lanes_t, jnp.zeros((8, 128), jnp.int32))
        is_shared = where_t > 0
        row_t = jnp.where(is_shared, (where_t >> 7) - 1, rows_t)
        if t == 3:
            row_t = jnp.where(sublane < 3, row_t, 99)
        row_scr[pl.ds(8 * t, 8), :] = row_t
        lane_scr[pl.ds(8 * t, 8), :] = jnp.where(is_shared, where_t & 127, lanes_t)

    columns = jnp.transpose(lane_scr[...].astype(F32))
    lanes_all = lax.broadcasted_iota(jnp.int32, (128, 128), 1).astype(F32)
    for a in range(27):
        column = jnp.broadcast_to(columns[:, a : a + 1], (128, 128))
        hot_scr[pl.ds(128 * a, 128), :] = jnp.where(column == lanes_all, 1.0, 0.0).astype(BF16)

    for c in range(3):
        q_scr[0, pl.ds(16 * c, 16), :] = jnp.where(
            map_scr[...] > 0, 0.0, nodes_scr[pl.ds(16 * c, 16), :]
        )
    moment_scr[...] = jnp.zeros_like(moment_scr)

    def gather_inner(turn):
        for t in range(4):
            rows_t = row_scr[pl.ds(8 * t, 8), :]
            lanes_t = lane_scr[pl.ds(8 * t, 8), :]
            for c in range(3):
                part_scr[pl.ds(8 * t, 8), 128 * c : 128 * c + 128] = pick(
                    q_scr.at[turn], 16 * c + BASE, NODE_ROWS, BASE, rows_t, lanes_t, zero
                )

    gather_inner(0)
    send_sum(0, 1, wait_sum(0, 0))

    def moment(index, one, two):
        total = zero
        for c in range(3):
            for t in range(2):
                rows = pl.ds(16 * c + 8 * t, 8)
                total = total + weight_scr[pl.ds(8 * t, 8), :] * q_scr[one, rows, :] * q_scr[two, rows, :]
        moment_scr[pl.ds(index, 1), :] = jnp.sum(total, axis=0, keepdims=True)

    def write_basis(turn):
        for t in range(2):
            where_t = map_scr[pl.ds(8 * t, 8), :]
            rows_t, lanes_t = (where_t >> 7) - 1, where_t & 127
            for c in range(3):
                inner = q_scr[turn, pl.ds(16 * c + 8 * t, 8), :]
                value = pick(q_scr.at[turn], 16 * c, BASE, 0, rows_t, lanes_t, inner)
                for row in range(BASE if t == 0 else 0, 8):
                    start = 128 * (8 * t + row - BASE)
                    basis_scr[turn, pl.ds(c, 1), start : start + 128] = value[row : row + 1, :]

    def receive(turn, is_first):
        wait_halo(turn)
        lanes = lax.broadcasted_iota(jnp.int32, (1, 128), 1)
        for c in range(3):
            arrived = [recv_buf[turn, j, c] for j in range(PEERS)]
            for row in range(BASE):
                own = [j for j in range(PEERS) if PEER_ROW[j] == row]
                own.sort(key=lambda j: PEER_LANE[j])
                value = arrived[own[0]]
                for j in own[1:]:
                    value = jnp.where(lanes >= PEER_LANE[j], arrived[j], value)
                in_scr[pl.ds(8 * c + row, 1), :] = value
        for c in range(3):
            value = own_scr[pl.ds(8 * c, BASE), :] + in_scr[pl.ds(8 * c, BASE), :]
            if not is_first:
                before = q_scr[turn - 1, pl.ds(16 * c, BASE), :]
                scale = jnp.broadcast_to(scale_scr[0:1, :], (BASE, 128))
                value = value * scale + before * (DAMPING * scale - 1.0)
            q_scr[turn, pl.ds(16 * c, BASE), :] = value

    def stresses(turn):
        for t in range(4):
            rows_t = row_scr[pl.ds(8 * t, 8), :]
            lanes_t = lane_scr[pl.ds(8 * t, 8), :]
            for c in range(3):
                u_scr[pl.ds(8 * t, 8), 128 * c : 128 * c + 128] = pick(
                    q_scr.at[turn],
                    16 * c,
                    BASE,
                    0,
                    rows_t,
                    lanes_t,
                    part_scr[pl.ds(8 * t, 8), 128 * c : 128 * c + 128],
                )
        high, mid, low = parts_of(u_scr[...])
        right = jnp.concatenate([high, mid, low, high, mid, high], axis=0).astype(BF16)
        g_scr[...] = jnp.dot(first_ref[0:96, :], right, preferred_element_type=F32)
        energy = zero
        for t in range(2):
            grads = [
                g_scr[32 * (n % 3) + 16 * t : 32 * (n % 3) + 16 * t + 16, 128 * (n // 3) : 128 * (n // 3) + 128]
                for n in range(9)
            ]
            for m in range(9):
                total = h_scr[packed_index(m, 0), pl.ds(16 * t, 16), :] * grads[0]
                for n in range(1, 9):
                    total = total + h_scr[packed_index(m, n), pl.ds(16 * t, 16), :] * grads[n]
                product = total * grads[m]
                energy = energy + product[0:8] + product[8:16]
                for p, part in enumerate(parts_of(total)):
                    row = 96 * p + 32 * (m % 3) + 16 * t
                    s_scr[row : row + 16, 128 * (m // 3) : 128 * (m // 3) + 128] = part.astype(BF16)
        return energy

    def terms():
        blocks = jnp.dot(second_ref[...], s_scr[...], preferred_element_type=F32)
        summed = blocks[0:32] + blocks[32:64] + blocks[64:96]
        for p, part in enumerate(parts_of(summed)):
            t_scr[p] = part

    def term(p, a, c, height):
        row = t_scr[p, pl.ds(a, 1), 128 * c : 128 * c + 128]
        return jnp.broadcast_to(row, (height, 128))

    def by_lane(left):
        summed = None
        for a in range(0, 27, 4):
            part = jnp.dot(
                jnp.concatenate(left[a : a + 4], axis=1),
                hot_scr[128 * a : 128 * min(a + 4, 27), :],
                preferred_element_type=F32,
            )
            summed = part if summed is None else summed + part
        return summed

    def scatter_shared(turn):
        order = [(c, p) for c in range(3) for p in range(3)]
        upper = sublane < BASE
        numbers = sublane & (BASE - 1)
        left = []
        for a in range(27):
            mask = spread(row_scr, a) == numbers
            tiles = []
            for i in range(0, 9, 2):
                value = term(order[i][1], a, order[i][0], 8)
                if i < 8:
                    other = term(order[i + 1][1], a, order[i + 1][0], 8)
                    tiles.append(jnp.where(mask, jnp.where(upper, value, other), 0.0))
                else:
                    tiles.append(jnp.where(mask & upper, value, 0.0))
            tiles.append(zero)
            left.append(jnp.concatenate(tiles, axis=0).astype(BF16))
        summed = by_lane(left)
        for c in range(3):
            own_scr[pl.ds(8 * c, BASE), :] = (
                summed[12 * c : 12 * c + 4]
                + summed[12 * c + 4 : 12 * c + 8]
                + summed[12 * c + 8 : 12 * c + 12]
            )
        fill_message(turn + 1)
        send_halo(turn + 1)

    def scatter_inner():
        left = []
        for a in range(27):
            mask = jnp.broadcast_to(row_scr[pl.ds(a, 1), :], (16, 128)) == sublane16
            tiles = [jnp.where(mask, term(p, a, c, 16), 0.0) for c in range(3) for p in range(3)]
            left.append(jnp.concatenate(tiles, axis=0).astype(BF16))
        summed = by_lane(left)
        for c in range(3):
            inner_scr[pl.ds(16 * c, 16), :] = (
                summed[48 * c : 48 * c + 16]
                + summed[48 * c + 16 : 48 * c + 32]
                + summed[48 * c + 32 : 48 * c + 48]
            )

    def inner_rows(turn):
        scale = jnp.broadcast_to(scale_scr[0:1, :], (16, 128))
        for c in range(3):
            rows = pl.ds(16 * c, 16)
            q_scr[turn + 1, rows, :] = inner_scr[rows, :] * scale + q_scr[turn, rows, :] * (
                DAMPING * scale - 1.0
            )

    def turn_of(turn, is_first):
        receive(turn, is_first)
        stresses(turn)
        terms()
        scatter_shared(turn)
        scatter_inner()
        moment(2 * turn, turn, turn)
        if is_first:
            write_basis(turn)
            row = wait_sum(0, 1)
            total, squares = lane_of(row, 0), lane_of(row, 1)
            scale_scr[0:1, :] = 1.0 / (DAMPING + SHIFT_SCALE * squares / total)
            inner_rows(turn)
            gather_inner(turn + 1)
        else:
            inner_rows(turn)
            gather_inner(turn + 1)
            moment(2 * turn - 1, turn - 1, turn)
            write_basis(turn)

    turn_of(0, True)

    def body(turn, carry):
        turn_of(turn, False)
        return carry

    lax.fori_loop(1, ITERS - 1, body, 0)

    last = ITERS - 1
    receive(last, False)
    moment(2 * last - 1, last - 1, last)
    moment(2 * last, last, last)
    known = row_of(moment_scr[...])
    energy = jnp.sum(stresses(last), axis=0, keepdims=True)
    total = jnp.sum(energy, axis=1, keepdims=True)
    send_sum(1, 0, jnp.where(lane[0:1, :] == 2 * last + 1, total, known))
    terms()
    scatter_shared(last)
    scatter_inner()
    send_sum(1, 1, wait_sum(1, 0))
    inner_rows(last)
    write_basis(last)
    receive(ITERS, False)
    write_basis(ITERS)
    row = wait_sum(1, 1)

    scale = scale_scr[0:1, :]
    m = [lane_of(row, k) for k in range(2 * ITERS)]
    m[2 * last + 1] = m[2 * last + 1] * scale + m[2 * last] * (DAMPING * scale - 1.0)
    low = [[None] * ITERS for _ in range(ITERS)]
    low_d = [[None] * ITERS for _ in range(ITERS)]
    inverse = [None] * ITERS
    right = [None] * ITERS
    for j in range(ITERS):
        pivot = m[2 * j]
        value = m[j + ITERS]
        for k in range(j):
            pivot = pivot - low[j][k] * low_d[j][k]
            value = value - low[j][k] * right[k]
        inverse[j] = 1.0 / pivot
        right[j] = value
        for i in range(j + 1, ITERS):
            entry = m[i + j]
            for k in range(j):
                entry = entry - low[i][k] * low_d[j][k]
            low_d[i][j] = entry
            low[i][j] = entry * inverse[j]
    coef = [None] * ITERS
    for i in reversed(range(ITERS)):
        value = right[i] * inverse[i]
        for k in range(i + 1, ITERS):
            value = value - low[k][i] * coef[k]
        coef[i] = value
    norm = -1.0
    for i in range(ITERS):
        norm = norm - coef[i] if i % 2 == 0 else norm + coef[i]
    by_norm = 1.0 / norm
    rest = [-value * by_norm for value in coef] + [by_norm]
    steps = [1.0 - rest[0]]
    for i in range(1, ITERS):
        steps.append(-rest[i] - steps[-1])
    rest = [jnp.broadcast_to(value, (8, 128)) for value in rest]
    steps = [jnp.broadcast_to(value * scale, (8, 128)) for value in steps]
    for r in range(NODE_ROWS):
        width = min(128, NODES - 128 * r)
        tiles = [basis_scr[i, :, 128 * r : 128 * r + 128] for i in range(ITERS + 1)]
        newton = tiles[0] * steps[0]
        for i in range(1, ITERS):
            newton = newton + tiles[i] * steps[i]
        left = tiles[0] * rest[0]
        for i in range(1, ITERS + 1):
            left = left + tiles[i] * rest[i]
        out_ref[0, :, 128 * r : 128 * r + width] = newton[0:3, 0:width]
        out_ref[1, :, 128 * r : 128 * r + width] = left[0:3, 0:width]

    for turn in range(ITERS + 1):
        pltpu.make_async_copy(recv_buf.at[turn], recv_buf.at[turn], halo_send.at[turn]).wait()
    for which in range(2):
        for stage in range(2):
            arrived = sum_in[stage].at[which]
            pltpu.make_async_copy(arrived, arrived, sum_send.at[2 * which + stage]).wait()


def shards(count, rhs_partial, connectivity, hessians, shared_nodes, owner):
    first, second = tables()
    sizes = [len(masks) for masks in stage_masks(count)]
    vmem = pltpu.VMEM
    out = pl.pallas_call(
        functools.partial(kernel, count),
        out_shape=vmem((2, 3, NODES), F32),
        in_specs=[pl.BlockSpec(memory_space=pltpu.HBM)] * 7,
        out_specs=pl.BlockSpec(memory_space=vmem),
        scratch_shapes=[
            vmem((3, NODES), F32),
            vmem((27, 128), jnp.int32),
            vmem((27, 45, 128), BF16),
            vmem((8, SHARE), jnp.int32),
            vmem((NODES,), jnp.int32),
            vmem(first.shape, BF16),
            vmem(second.shape, BF16),
            pltpu.SemaphoreType.DMA((7,)),
            vmem((48, 128), F32),
            vmem((16, 128), F32),
            vmem((8, 128), jnp.int32),
            vmem((16, 128), jnp.int32),
            vmem((32, 128), jnp.int32),
            vmem((32, 128), jnp.int32),
            vmem((32, 128), jnp.int32),
            vmem((27 * 128, 128), BF16),
            vmem((48 * 33, 128), F32),
            vmem((45, 32, 128), F32),
            vmem((ITERS + 1, 3 * ROWS, 128), F32),
            vmem((24, 128), F32),
            vmem((48, 128), F32),
            vmem((24, 128), F32),
            vmem((32, 384), F32),
            vmem((32, 384), F32),
            vmem((96, 384), F32),
            vmem((288, 384), BF16),
            vmem((3, 32, 384), F32),
            vmem((ROWS, 128), F32),
            vmem((16, 128), F32),
            vmem((8, 128), F32),
            vmem((ITERS + 1, 8, NODE_ROWS * 128), F32),
            vmem((ITERS + 1, BASE, 3, 1, 128), F32),
            vmem((ITERS + 1, PEERS, 3, 1, 128), F32),
            vmem((4, 1, 128), F32),
            vmem((2, sizes[0], 1, 128), F32),
            vmem((2, sizes[1], 1, 128), F32),
            pltpu.SemaphoreType.DMA((ITERS + 1,)),
            pltpu.SemaphoreType.DMA((ITERS + 1,)),
            pltpu.SemaphoreType.DMA((4,)),
            pltpu.SemaphoreType.DMA((4,)),
        ],
        compiler_params=pltpu.CompilerParams(collective_id=0, has_side_effects=True),
        name="newton_cg",
    )(
        rhs_partial,
        connectivity,
        jnp.transpose(hessians, (1, 0, 2)),
        shared_nodes,
        owner,
        jnp.asarray(first),
        jnp.asarray(second),
    )
    return out[0], out[1]


def solution(mesh):
    in_specs = (
        P(None, "parts"),
        P(None, "parts"),
        P(None, None, "parts"),
        P(None, "parts"),
        P("parts"),
    )
    out_specs = (P(None, "parts"), P(None, "parts"))
    return jax.shard_map(
        functools.partial(shards, mesh.shape["parts"]),
        mesh=mesh,
        in_specs=in_specs,
        out_specs=out_specs,
        check_vma=False,
    )
```

```python
import functools

import jax
import jax.numpy as jnp
import ml_dtypes
import numpy as np
from jax import lax
from jax.experimental import pallas as pl
from jax.experimental.pallas import tpu as pltpu
from jax.sharding import PartitionSpec as P

ITERS = 5
DAMPING = 2.0
MESH = pl.DeviceIdType.MESH
F32 = jnp.float32
BF16 = jnp.bfloat16

NODES = 1445
NODE_ROWS = 12
BASE = 4
ROWS = BASE + NODE_ROWS
PEERS = 8
SHARE = 34
PEER_ROW = [0, 0, 0, 2, 3, 1, 1, 1]
PEER_LANE = [0, 40, 80, 0, 0, 80, 40, 0]
SEND_ORDER = [0, 7, 1, 6, 2, 5, 3, 4]
SHIFT_SCALE = 0.045


def shape_table():
    points = np.array([-np.sqrt(0.6), 0.0, np.sqrt(0.6)])
    values = np.stack(
        [points * (points - 1.0) / 2.0, 1.0 - points * points, points * (points + 1.0) / 2.0],
        axis=1,
    )
    slopes = np.stack([points - 0.5, -2.0 * points, points + 0.5], axis=1)
    result = np.zeros((27, 3, 27))
    for direction in range(3):
        factors = [slopes if axis_index == direction else values for axis_index in range(3)]
        product = (
            factors[0][:, None, None, :, None, None]
            * factors[1][None, :, None, None, :, None]
            * factors[2][None, None, :, None, None, :]
        )
        result[:, direction, :] = product.reshape(27, 27)
    return result


def three_parts(table):
    rest = table.astype(np.float32)
    parts = []
    for _ in range(3):
        part = rest.astype(ml_dtypes.bfloat16)
        parts.append(part)
        rest = rest - part.astype(np.float32)
    return parts


def tables():
    table = shape_table()
    forward = np.zeros((3, 32, 32))
    forward[:, :27, :27] = table.transpose(1, 0, 2)
    high, mid, low = three_parts(forward.reshape(96, 32))
    first = np.concatenate([high, high, high, mid, mid, low], axis=1)
    weights = np.einsum("qda,qfa->dfq", table, table)
    row = np.zeros((16, 6, 32))
    for pair, (one, two) in enumerate(PAIRS):
        row[0, pair, :27] = weights[one, two] * (1.0 if one == two else 2.0)
    first = np.concatenate([first, row.reshape(16, 192).astype(ml_dtypes.bfloat16)], axis=0)
    high, mid, low = three_parts(forward.transpose(2, 0, 1).reshape(32, 96))
    zero = np.zeros_like(high)
    second = np.concatenate(
        [
            np.concatenate([high, high, high], axis=1),
            np.concatenate([mid, mid, zero], axis=1),
            np.concatenate([low, zero, zero], axis=1),
        ],
        axis=0,
    )
    return first, second


PAIRS = [(0, 0), (0, 1), (0, 2), (1, 1), (1, 2), (2, 2)]


def packed_index(row_index, col_index):
    first = min(row_index, col_index)
    second = max(row_index, col_index)
    return first * 9 - first * (first - 1) // 2 + (second - first)


def peer_offsets(count):
    half = count // 2
    return [offset - half for offset in range(half)] + [offset + 1 for offset in range(half)]


def links(mask):
    ring = [0, 1, 2, 3, 4, 3, 2, 3]
    return ring[(mask >> 1) & 7] + ring[(mask >> 4) & 7] + [0, 1, 2, 1][(mask >> 7) & 3]


def stage_masks(count):
    bits = count.bit_length() - 1
    low = 1 << min(4, bits - 1)
    masks = [list(range(1, low)), [low * k for k in range(1, count // low)]]
    return [sorted(stage, key=lambda mask: -links(mask)) for stage in masks]


def parts_of(value):
    high = value.astype(BF16).astype(F32)
    rest = value - high
    mid = rest.astype(BF16).astype(F32)
    return high, mid, (rest - mid).astype(BF16).astype(F32)


def lane_of(row, lane):
    return jnp.broadcast_to(row[:, lane : lane + 1], (1, 128))


def spread(ref, row):
    return jnp.broadcast_to(ref[pl.ds(row, 1), :], (8, 128))


def pick(ref, base, count, first, rows, lanes, start):
    result = start
    for row in range(count):
        found = jnp.take_along_axis(spread(ref, base + row), lanes, axis=1)
        result = jnp.where(rows == first + row, found, result)
    return result


def kernel(
    count,
    rhs_hbm,
    conn_hbm,
    hess_hbm,
    shared_hbm,
    owner_hbm,
    first_hbm,
    second_hbm,
    out_ref,
    rhs_ref,
    conn_ref,
    hess_ref,
    shared_ref,
    owner_ref,
    first_ref,
    second_ref,
    load_sem,
    nodes_scr,
    owner_scr,
    shared_scr,
    map_scr,
    conn_scr,
    row_scr,
    lane_scr,
    hot_scr,
    wide_scr,
    h_scr,
    q_scr,
    own_scr,
    inner_scr,
    in_scr,
    part_scr,
    u_scr,
    g_scr,
    s_scr,
    t_scr,
    weight_scr,
    moment_scr,
    scale_scr,
    basis_scr,
    send_buf,
    recv_buf,
    sum_out,
    sum_in0,
    sum_in1,
    halo_send,
    halo_recv,
    sum_send,
    sum_recv,
):
    me = lax.axis_index("parts")
    peers = [(me + offset) & (count - 1) for offset in peer_offsets(PEERS)]
    stages = [[me ^ mask for mask in masks] for masks in stage_masks(count)]
    sum_in = [sum_in0, sum_in1]

    barrier = pltpu.get_barrier_semaphore()
    everyone = peers + stages[0] + stages[1]
    for other in everyone:
        pl.semaphore_signal(barrier, inc=1, device_id=(other,), device_id_type=MESH)

    loads = [
        pltpu.make_async_copy(source, target, load_sem.at[i])
        for i, (source, target) in enumerate(
            [
                (rhs_hbm, rhs_ref),
                (shared_hbm, shared_ref),
                (owner_hbm, owner_ref),
                (hess_hbm, hess_ref),
                (first_hbm, first_ref),
                (conn_hbm, conn_ref),
                (second_hbm, second_ref),
            ]
        )
    ]
    for load in loads:
        load.start()

    sublane = lax.broadcasted_iota(jnp.int32, (8, 128), 0)
    lane = lax.broadcasted_iota(jnp.int32, (8, 128), 1)
    sublane16 = lax.broadcasted_iota(jnp.int32, (16, 128), 0)

    def send_halo(turn):
        for j in SEND_ORDER:
            pltpu.make_async_remote_copy(
                src_ref=send_buf.at[turn, PEER_ROW[j]],
                dst_ref=recv_buf.at[turn, PEERS - 1 - j],
                send_sem=halo_send.at[turn],
                recv_sem=halo_recv.at[turn],
                device_id=(peers[j],),
                device_id_type=MESH,
            ).start()

    def wait_halo(turn):
        pltpu.make_async_copy(recv_buf.at[turn], recv_buf.at[turn], halo_recv.at[turn]).wait()

    def send_sum(which, stage, row):
        slot = 2 * which + stage
        sum_out[slot] = row
        for k, other in enumerate(stages[stage]):
            pltpu.make_async_remote_copy(
                src_ref=sum_out.at[slot],
                dst_ref=sum_in[stage].at[which, k],
                send_sem=sum_send.at[slot],
                recv_sem=sum_recv.at[slot],
                device_id=(other,),
                device_id_type=MESH,
            ).start()

    def wait_sum(which, stage):
        slot = 2 * which + stage
        arrived = sum_in[stage].at[which]
        pltpu.make_async_copy(arrived, arrived, sum_recv.at[slot]).wait()
        terms = [sum_out[slot]] + [sum_in[stage][which, k] for k in range(len(stages[stage]))]
        while len(terms) > 1:
            terms = [sum(terms[i : i + 2]) for i in range(0, len(terms), 2)]
        return terms[0]

    nodes_scr[...] = jnp.zeros_like(nodes_scr)
    owner_scr[...] = jnp.zeros_like(owner_scr)
    for load in loads[0:3]:
        load.wait()
    for r in range(NODE_ROWS):
        width = min(128, NODES - 128 * r)
        for c in range(3):
            nodes_scr[pl.ds(16 * c + BASE + r, 1), 0:width] = rhs_ref[c : c + 1, 128 * r : 128 * r + width]
        owner_scr[pl.ds(BASE + r, 1), 0:width] = owner_ref[128 * r : 128 * r + width].reshape(1, width).astype(F32)
    shared_scr[...] = jnp.full((8, 128), NODES, jnp.int32)
    for j in range(PEERS):
        start = PEER_LANE[j]
        shared_scr[PEER_ROW[j] : PEER_ROW[j] + 1, start : start + SHARE] = shared_ref[j : j + 1, :]
    names = shared_scr[...]
    used = names < NODES
    name_rows, name_lanes = (names >> 7) + BASE, names & 127
    zero = jnp.zeros((8, 128), F32)
    for c in range(3):
        found = pick(nodes_scr, 16 * c + BASE, NODE_ROWS, BASE, name_rows, name_lanes, zero)
        own_scr[pl.ds(8 * c, 8), :] = jnp.where(used, found, 0.0)
    owned = pick(owner_scr, BASE, NODE_ROWS, BASE, name_rows, name_lanes, zero)
    shared_weight = jnp.where(used, owned, 0.0)

    def fill_message(turn):
        for c in range(3):
            for row in range(BASE):
                send_buf[turn, row, c] = own_scr[pl.ds(8 * c + row, 1), :]

    fill_message(0)
    pl.semaphore_wait(barrier, len(everyone))
    send_halo(0)

    for load in loads[3:]:
        load.wait()
    for q in range(27):
        wide_scr[48 * q : 48 * q + 45, :] = hess_ref[q].astype(F32)
    wide_scr[48 * 27 : 48 * 32, :] = jnp.zeros((48 * 5, 128), F32)
    for k in range(45):
        for t in range(4):
            h_scr[k, 8 * t : 8 * t + 8, :] = wide_scr[pl.ds(48 * 8 * t + k, 8, stride=48), :]
    sums = []
    for one, two in PAIRS:
        total = h_scr[packed_index(one, two)]
        for i in range(1, 3):
            total = total + h_scr[packed_index(3 * i + one, 3 * i + two)]
        sums.append(total)
    stacked = jnp.concatenate(sums, axis=0).astype(BF16)
    traces = jnp.dot(first_ref[96:112, :], stacked, preferred_element_type=F32)[0:1, :]

    def row_of(values):
        totals = jnp.sum(values, axis=1, keepdims=True)
        rows = lax.broadcasted_iota(jnp.int32, values.shape, 0)
        lanes = lax.broadcasted_iota(jnp.int32, values.shape, 1)
        return jnp.sum(jnp.where(rows == lanes, totals, 0.0), axis=0, keepdims=True)

    both = jnp.where(sublane == 0, traces, jnp.where(sublane == 1, traces * traces, 0.0))
    send_sum(0, 0, row_of(both))

    found = jnp.zeros((32, 128), F32)
    for j in range(BASE):
        rows_j = jnp.broadcast_to(jnp.where(used, name_rows, 99)[j : j + 1, :], (16, 128))
        lanes_j = jnp.broadcast_to(name_lanes[j : j + 1, :], (128, 128))
        hit = rows_j == sublane16
        slot = lax.broadcasted_iota(jnp.int32, (16, 128), 1).astype(F32)
        left = jnp.concatenate(
            [jnp.where(hit, float(j + 1), 0.0), jnp.where(hit, slot, 0.0)], axis=0
        )
        right = jnp.where(
            lanes_j == lax.broadcasted_iota(jnp.int32, (128, 128), 0), 1.0, 0.0
        )
        found = found + lax.dot_general(
            left.astype(BF16),
            right.astype(BF16),
            (((1,), (1,)), ((), ())),
            preferred_element_type=F32,
        )
    map_scr[...] = (128.0 * found[0:16] + found[16:32]).astype(jnp.int32)
    others = jnp.where(map_scr[...] > 0, 0.0, owner_scr[...])
    weight_scr[0:8, :] = others[0:8] + shared_weight
    weight_scr[8:16, :] = others[8:16]

    conn_scr[...] = jnp.zeros_like(conn_scr)
    conn_scr[0:27, :] = conn_ref[...]
    for t in range(4):
        names_t = conn_scr[pl.ds(8 * t, 8), :]
        rows_t, lanes_t = (names_t >> 7) + BASE, names_t & 127
        where_t = pick(map_scr, BASE, NODE_ROWS, BASE, rows_t, lanes_t, jnp.zeros((8, 128), jnp.int32))
        is_shared = where_t > 0
        row_t = jnp.where(is_shared, (where_t >> 7) - 1, rows_t)
        if t == 3:
            row_t = jnp.where(sublane < 3, row_t, 99)
        row_scr[pl.ds(8 * t, 8), :] = row_t
        lane_scr[pl.ds(8 * t, 8), :] = jnp.where(is_shared, where_t & 127, lanes_t)

    columns = jnp.transpose(lane_scr[...].astype(F32))
    lanes_all = lax.broadcasted_iota(jnp.int32, (128, 128), 1).astype(F32)
    for a in range(27):
        column = jnp.broadcast_to(columns[:, a : a + 1], (128, 128))
        hot_scr[pl.ds(128 * a, 128), :] = jnp.where(column == lanes_all, 1.0, 0.0).astype(BF16)

    for c in range(3):
        q_scr[0, pl.ds(16 * c, 16), :] = jnp.where(
            map_scr[...] > 0, 0.0, nodes_scr[pl.ds(16 * c, 16), :]
        )
    moment_scr[...] = jnp.zeros_like(moment_scr)

    def gather_inner(turn):
        for t in range(4):
            rows_t = row_scr[pl.ds(8 * t, 8), :]
            lanes_t = lane_scr[pl.ds(8 * t, 8), :]
            for c in range(3):
                part_scr[pl.ds(8 * t, 8), 128 * c : 128 * c + 128] = pick(
                    q_scr.at[turn], 16 * c + BASE, NODE_ROWS, BASE, rows_t, lanes_t, zero
                )

    gather_inner(0)
    send_sum(0, 1, wait_sum(0, 0))

    def moment(index, one, two):
        total = zero
        for c in range(3):
            for t in range(2):
                rows = pl.ds(16 * c + 8 * t, 8)
                total = total + weight_scr[pl.ds(8 * t, 8), :] * q_scr[one, rows, :] * q_scr[two, rows, :]
        moment_scr[pl.ds(index, 1), :] = jnp.sum(total, axis=0, keepdims=True)

    def write_basis(turn):
        for t in range(2):
            where_t = map_scr[pl.ds(8 * t, 8), :]
            rows_t, lanes_t = (where_t >> 7) - 1, where_t & 127
            for c in range(3):
                inner = q_scr[turn, pl.ds(16 * c + 8 * t, 8), :]
                value = pick(q_scr.at[turn], 16 * c, BASE, 0, rows_t, lanes_t, inner)
                for row in range(BASE if t == 0 else 0, 8):
                    start = 128 * (8 * t + row - BASE)
                    basis_scr[turn, pl.ds(c, 1), start : start + 128] = value[row : row + 1, :]

    def receive(turn, is_first):
        wait_halo(turn)
        lanes = lax.broadcasted_iota(jnp.int32, (1, 128), 1)
        for c in range(3):
            arrived = [recv_buf[turn, j, c] for j in range(PEERS)]
            for row in range(BASE):
                own = [j for j in range(PEERS) if PEER_ROW[j] == row]
                own.sort(key=lambda j: PEER_LANE[j])
                value = arrived[own[0]]
                for j in own[1:]:
                    value = jnp.where(lanes >= PEER_LANE[j], arrived[j], value)
                in_scr[pl.ds(8 * c + row, 1), :] = value
        for c in range(3):
            value = own_scr[pl.ds(8 * c, BASE), :] + in_scr[pl.ds(8 * c, BASE), :]
            if not is_first:
                before = q_scr[turn - 1, pl.ds(16 * c, BASE), :]
                scale = jnp.broadcast_to(scale_scr[0:1, :], (BASE, 128))
                value = value * scale + before * (DAMPING * scale - 1.0)
            q_scr[turn, pl.ds(16 * c, BASE), :] = value

    def stresses(turn):
        for t in range(4):
            rows_t = row_scr[pl.ds(8 * t, 8), :]
            lanes_t = lane_scr[pl.ds(8 * t, 8), :]
            for c in range(3):
                u_scr[pl.ds(8 * t, 8), 128 * c : 128 * c + 128] = pick(
                    q_scr.at[turn],
                    16 * c,
                    BASE,
                    0,
                    rows_t,
                    lanes_t,
                    part_scr[pl.ds(8 * t, 8), 128 * c : 128 * c + 128],
                )
        high, mid, low = parts_of(u_scr[...])
        right = jnp.concatenate([high, mid, low, high, mid, high], axis=0).astype(BF16)
        g_scr[...] = jnp.dot(first_ref[0:96, :], right, preferred_element_type=F32)
        energy = zero
        for t in range(2):
            grads = [
                g_scr[32 * (n % 3) + 16 * t : 32 * (n % 3) + 16 * t + 16, 128 * (n // 3) : 128 * (n // 3) + 128]
                for n in range(9)
            ]
            for m in range(9):
                total = h_scr[packed_index(m, 0), pl.ds(16 * t, 16), :] * grads[0]
                for n in range(1, 9):
                    total = total + h_scr[packed_index(m, n), pl.ds(16 * t, 16), :] * grads[n]
                product = total * grads[m]
                energy = energy + product[0:8] + product[8:16]
                for p, part in enumerate(parts_of(total)):
                    row = 96 * p + 32 * (m % 3) + 16 * t
                    s_scr[row : row + 16, 128 * (m // 3) : 128 * (m // 3) + 128] = part.astype(BF16)
        return energy

    def terms():
        blocks = jnp.dot(second_ref[...], s_scr[...], preferred_element_type=F32)
        summed = blocks[0:32] + blocks[32:64] + blocks[64:96]
        for p, part in enumerate(parts_of(summed)):
            t_scr[p] = part

    def term(p, a, c, height):
        row = t_scr[p, pl.ds(a, 1), 128 * c : 128 * c + 128]
        return jnp.broadcast_to(row, (height, 128))

    def by_lane(left):
        summed = None
        for a in range(0, 27, 4):
            part = jnp.dot(
                jnp.concatenate(left[a : a + 4], axis=1),
                hot_scr[128 * a : 128 * min(a + 4, 27), :],
                preferred_element_type=F32,
            )
            summed = part if summed is None else summed + part
        return summed

    def scatter_shared(turn):
        order = [(c, p) for c in range(3) for p in range(3)]
        upper = sublane < BASE
        numbers = sublane & (BASE - 1)
        order_a = [a for a in range(27) if a not in (12, 13)] + [12]
        left = []
        for a in order_a:
            mask = spread(row_scr, a) == numbers
            tiles = []
            for i in range(0, 9, 2):
                value = term(order[i][1], a, order[i][0], 8)
                if i < 8:
                    other = term(order[i + 1][1], a, order[i + 1][0], 8)
                    tiles.append(jnp.where(mask, jnp.where(upper, value, other), 0.0))
                else:
                    tiles.append(jnp.where(mask & upper, value, 0.0))
            tiles.append(zero)
            left.append(jnp.concatenate(tiles, axis=0).astype(BF16))
        summed = None
        for i in range(0, 26, 2):
            table = [hot_scr[128 * a : 128 * a + 128, :] for a in order_a[i : i + 2]]
            part = jnp.dot(
                jnp.concatenate(left[i : i + 2], axis=1),
                jnp.concatenate(table, axis=0),
                preferred_element_type=F32,
            )
            summed = part if summed is None else summed + part
        for c in range(3):
            own_scr[pl.ds(8 * c, BASE), :] = (
                summed[12 * c : 12 * c + 4]
                + summed[12 * c + 4 : 12 * c + 8]
                + summed[12 * c + 8 : 12 * c + 12]
            )
        fill_message(turn + 1)
        send_halo(turn + 1)

    def scatter_inner():
        left = []
        for a in range(27):
            mask = jnp.broadcast_to(row_scr[pl.ds(a, 1), :], (16, 128)) == sublane16
            tiles = [jnp.where(mask, term(p, a, c, 16), 0.0) for c in range(3) for p in range(3)]
            left.append(jnp.concatenate(tiles, axis=0).astype(BF16))
        summed = by_lane(left)
        for c in range(3):
            inner_scr[pl.ds(16 * c, 16), :] = (
                summed[48 * c : 48 * c + 16]
                + summed[48 * c + 16 : 48 * c + 32]
                + summed[48 * c + 32 : 48 * c + 48]
            )

    def inner_rows(turn):
        scale = jnp.broadcast_to(scale_scr[0:1, :], (16, 128))
        for c in range(3):
            rows = pl.ds(16 * c, 16)
            q_scr[turn + 1, rows, :] = inner_scr[rows, :] * scale + q_scr[turn, rows, :] * (
                DAMPING * scale - 1.0
            )

    def turn_of(turn, is_first):
        receive(turn, is_first)
        stresses(turn)
        terms()
        scatter_shared(turn)
        scatter_inner()
        moment(2 * turn, turn, turn)
        if is_first:
            write_basis(turn)
            row = wait_sum(0, 1)
            total, squares = lane_of(row, 0), lane_of(row, 1)
            scale_scr[0:1, :] = 1.0 / (DAMPING + SHIFT_SCALE * squares / total)
            inner_rows(turn)
            gather_inner(turn + 1)
        else:
            inner_rows(turn)
            gather_inner(turn + 1)
            moment(2 * turn - 1, turn - 1, turn)
            write_basis(turn)

    turn_of(0, True)

    def body(turn, carry):
        turn_of(turn, False)
        return carry

    lax.fori_loop(1, ITERS - 1, body, 0)

    last = ITERS - 1
    receive(last, False)
    moment(2 * last - 1, last - 1, last)
    moment(2 * last, last, last)
    known = row_of(moment_scr[...])
    energy = jnp.sum(stresses(last), axis=0, keepdims=True)
    total = jnp.sum(energy, axis=1, keepdims=True)
    send_sum(1, 0, jnp.where(lane[0:1, :] == 2 * last + 1, total, known))
    terms()
    scatter_shared(last)
    scatter_inner()
    send_sum(1, 1, wait_sum(1, 0))
    inner_rows(last)
    write_basis(last)
    receive(ITERS, False)
    write_basis(ITERS)
    row = wait_sum(1, 1)

    scale = scale_scr[0:1, :]
    m = [lane_of(row, k) for k in range(2 * ITERS)]
    m[2 * last + 1] = m[2 * last + 1] * scale + m[2 * last] * (DAMPING * scale - 1.0)
    low = [[None] * ITERS for _ in range(ITERS)]
    low_d = [[None] * ITERS for _ in range(ITERS)]
    inverse = [None] * ITERS
    right = [None] * ITERS
    for j in range(ITERS):
        pivot = m[2 * j]
        value = m[j + ITERS]
        for k in range(j):
            pivot = pivot - low[j][k] * low_d[j][k]
            value = value - low[j][k] * right[k]
        inverse[j] = 1.0 / pivot
        right[j] = value
        for i in range(j + 1, ITERS):
            entry = m[i + j]
            for k in range(j):
                entry = entry - low[i][k] * low_d[j][k]
            low_d[i][j] = entry
            low[i][j] = entry * inverse[j]
    coef = [None] * ITERS
    for i in reversed(range(ITERS)):
        value = right[i] * inverse[i]
        for k in range(i + 1, ITERS):
            value = value - low[k][i] * coef[k]
        coef[i] = value
    norm = -1.0
    for i in range(ITERS):
        norm = norm - coef[i] if i % 2 == 0 else norm + coef[i]
    by_norm = 1.0 / norm
    rest = [-value * by_norm for value in coef] + [by_norm]
    steps = [1.0 - rest[0]]
    for i in range(1, ITERS):
        steps.append(-rest[i] - steps[-1])
    rest = [jnp.broadcast_to(value, (8, 128)) for value in rest]
    steps = [jnp.broadcast_to(value * scale, (8, 128)) for value in steps]
    for r in range(NODE_ROWS):
        width = min(128, NODES - 128 * r)
        tiles = [basis_scr[i, :, 128 * r : 128 * r + 128] for i in range(ITERS + 1)]
        newton = tiles[0] * steps[0]
        for i in range(1, ITERS):
            newton = newton + tiles[i] * steps[i]
        left = tiles[0] * rest[0]
        for i in range(1, ITERS + 1):
            left = left + tiles[i] * rest[i]
        out_ref[0, :, 128 * r : 128 * r + width] = newton[0:3, 0:width]
        out_ref[1, :, 128 * r : 128 * r + width] = left[0:3, 0:width]

    for turn in range(ITERS + 1):
        pltpu.make_async_copy(recv_buf.at[turn], recv_buf.at[turn], halo_send.at[turn]).wait()
    for which in range(2):
        for stage in range(2):
            arrived = sum_in[stage].at[which]
            pltpu.make_async_copy(arrived, arrived, sum_send.at[2 * which + stage]).wait()


def shards(count, rhs_partial, connectivity, hessians, shared_nodes, owner):
    first, second = tables()
    sizes = [len(masks) for masks in stage_masks(count)]
    vmem = pltpu.VMEM
    out = pl.pallas_call(
        functools.partial(kernel, count),
        out_shape=vmem((2, 3, NODES), F32),
        in_specs=[pl.BlockSpec(memory_space=pltpu.HBM)] * 7,
        out_specs=pl.BlockSpec(memory_space=vmem),
        scratch_shapes=[
            vmem((3, NODES), F32),
            vmem((27, 128), jnp.int32),
            vmem((27, 45, 128), BF16),
            vmem((8, SHARE), jnp.int32),
            vmem((NODES,), jnp.int32),
            vmem(first.shape, BF16),
            vmem(second.shape, BF16),
            pltpu.SemaphoreType.DMA((7,)),
            vmem((48, 128), F32),
            vmem((16, 128), F32),
            vmem((8, 128), jnp.int32),
            vmem((16, 128), jnp.int32),
            vmem((32, 128), jnp.int32),
            vmem((32, 128), jnp.int32),
            vmem((32, 128), jnp.int32),
            vmem((27 * 128, 128), BF16),
            vmem((48 * 33, 128), F32),
            vmem((45, 32, 128), F32),
            vmem((ITERS + 1, 3 * ROWS, 128), F32),
            vmem((24, 128), F32),
            vmem((48, 128), F32),
            vmem((24, 128), F32),
            vmem((32, 384), F32),
            vmem((32, 384), F32),
            vmem((96, 384), F32),
            vmem((288, 384), BF16),
            vmem((3, 32, 384), F32),
            vmem((ROWS, 128), F32),
            vmem((16, 128), F32),
            vmem((8, 128), F32),
            vmem((ITERS + 1, 8, NODE_ROWS * 128), F32),
            vmem((ITERS + 1, BASE, 3, 1, 128), F32),
            vmem((ITERS + 1, PEERS, 3, 1, 128), F32),
            vmem((4, 1, 128), F32),
            vmem((2, sizes[0], 1, 128), F32),
            vmem((2, sizes[1], 1, 128), F32),
            pltpu.SemaphoreType.DMA((ITERS + 1,)),
            pltpu.SemaphoreType.DMA((ITERS + 1,)),
            pltpu.SemaphoreType.DMA((4,)),
            pltpu.SemaphoreType.DMA((4,)),
        ],
        compiler_params=pltpu.CompilerParams(collective_id=0, has_side_effects=True),
        name="newton_cg",
    )(
        rhs_partial,
        connectivity,
        jnp.transpose(hessians, (1, 0, 2)),
        shared_nodes,
        owner,
        jnp.asarray(first),
        jnp.asarray(second),
    )
    return out[0], out[1]


def solution(mesh):
    in_specs = (
        P(None, "parts"),
        P(None, "parts"),
        P(None, None, "parts"),
        P(None, "parts"),
        P("parts"),
    )
    out_specs = (P(None, "parts"), P(None, "parts"))
    return jax.shard_map(
        functools.partial(shards, mesh.shape["parts"]),
        mesh=mesh,
        in_specs=in_specs,
        out_specs=out_specs,
        check_vma=False,
    )
```
